128 devices in a mesh: grp: 4 (over y_lo, core), col: 32 (over x, y_hi, z).
Axes of the slice: x: 4, y: 4 (y_hi: 2, y_lo: 2; y = y_hi * 2 + y_lo), z: 4, core: 2. Of those that a mesh axis runs over, the one named last changes fastest.
Arguments:
- amplitudes: bfloat16 [768, 262144], P(('grp', 'col')), may hold values from -6 to 6
- integrals: bfloat16 [4096, 262144], P('grp', 'col'), may hold values from -0.01171875 to 0.01171875
Outputs:
- ladder: float32 [768, 4096], P('col', 'grp')
The draws below stay inside these ranges and needn't reach their ends.
All inputs are finite; a program needn't handle non-finite values.
Results may differ from the reference program's by a relative error of at most 0.0003.
Values may be sent and summed in bfloat16 or wider, within the bound.
A program may use at most 128 MiB of HBM per device.

```python
import jax
import jax.numpy as jnp
from jax import lax

OPAN = 768
VPAIRS = 262144
AB = 4096


def shard_levels(stream_key, dims, shards, smallest, high):
    def one(axis_at, shards_of):
        steps = jax.random.uniform(jax.random.fold_in(jax.random.fold_in(stream_key, 6), axis_at), (shards_of,), jnp.float32, smallest / len(shards), high / len(shards))
        return jnp.repeat(jnp.exp(steps), dims[axis_at] // shards_of).reshape((-1,) + (1,) * (len(dims) - axis_at - 1))

    factor_of = one(*shards[0])
    for cut in shards[1:]:
        factor_of = factor_of * one(*cut)
    return factor_of


def scatter_about(key, dims, deviation, most, pieces=(), kind=jnp.bfloat16):
    values = jax.random.normal(key, dims, jnp.float32) * deviation
    if len(pieces) > 0:
        values = shard_levels(key, dims, pieces, -0.22, 0.18) * values
    return jnp.clip(values, min=-most, max=most).astype(kind)


def setup_inputs(seed: int = 0) -> dict:
    arg_keys = jax.random.split(jax.random.key(seed), 3)
    amplitudes = scatter_about(arg_keys[0], (OPAN, VPAIRS), 1.0, 6.0, ((0, 128),))
    integrals = scatter_about(arg_keys[1], (AB, VPAIRS), VPAIRS ** -0.5, 0.01171875, ((0, 4), (1, 32)))
    return dict(amplitudes=amplitudes, integrals=integrals)


def reference(amplitudes, integrals):
    products = lax.dot_general(amplitudes, integrals, (((1,), (1,)), ((), ())), preferred_element_type=jnp.float32)
    return 0.5 * products
```

```python
import jax
import jax.numpy as jnp
from jax import lax
from jax.experimental import pallas as pl
from jax.experimental.pallas import tpu as pltpu
from jax.sharding import PartitionSpec as P

MESH = pl.DeviceIdType.MESH
ROWS = 6
BLOCK = 8 * ROWS
STEP = 4 * BLOCK
STEPS = 4
PIECE = 24
KPARTS = 4
LEVEL = 99


def device(x, y, z, s):
    return ((y % 2) * 2 + s, (x * 2 + y // 2) * 4 + z)


def across(y):
    return (y + 3 + 2 * (y % 2)) % 4


def kernel(amp, integrals_hbm, out, integrals, landed, wide, panel, parts, from_z, reduced, from_xy,
           load_sem, send_sem, land_sem, pair_send, sib_send, block_sem, z_send, z_recv, xy_send, xy_recv):
    g = lax.axis_index("grp")
    c = lax.axis_index("col")
    x, y, z, s = c // 8, (c // 4) % 2 * 2 + g // 2, c % 4, g % 2
    y_hi, y_lo = y // 2, y % 2
    kind = (y_lo + y_hi) % 2
    cols = integrals.shape[1]
    part = cols // KPARTS
    core = x % 2
    own = jnp.where(s == core, 1, 0)
    pair = device(x, y + 1 - 2 * y_lo, z, s)
    sibling = device(x, y, z, 1 - s)

    load = pltpu.make_async_copy(integrals_hbm, integrals, load_sem)
    load.start()

    bar = pltpu.get_barrier_semaphore()

    def greet(i, _):
        src_x = 2 * (i % 2) + s
        src_y = jnp.where((i // 2) % 2 == 0, y, across(y))
        src_z = (i // 4) % 4
        src_s = i // 16
        other = jnp.logical_not((src_x == x) & (src_y == y) & (src_z == z) & (src_s == s))

        @pl.when(other)
        def _():
            pl.semaphore_signal(bar, inc=1, device_id=device(src_x, src_y, src_z, src_s), device_id_type=MESH)

        return 0

    lax.fori_loop(0, 32, greet, 0)
    pl.semaphore_signal(bar, inc=1, device_id=pair, device_id_type=MESH)
    pl.semaphore_signal(bar, inc=1, device_id=sibling, device_id_type=MESH)
    for d in range(1, 4):
        pl.semaphore_signal(bar, inc=1, device_id=device(x, y, (z + d) % 4, s), device_id_type=MESH)
    for d in range(1, 8):
        pl.semaphore_signal(bar, inc=1, device_id=device((x + d % 4) % 4, (y + 2 * (d // 4)) % 4, z, s), device_id_type=MESH)
    pl.semaphore_wait(bar, 44 - own)

    my_step = s * 2 + x // 2

    def send_all():
        def one(n, _):
            k, i = n // 32, n % 32
            j, m = i // 2, i % 2
            dx = j % 4
            dz = (j // 4 + j) % 4
            to_x = jnp.where(m == 0, x + dx, x - dx + 4) % 4
            to_z = jnp.where(m == 0, z + dz, z - dz + 4) % 4
            to_y = jnp.where(m == 0, y, across(y))
            to_col = (to_x * 2 + to_y // 2) * 4 + to_z
            src = amp.at[:, pl.ds(pl.multiple_of(to_col * cols + k * part, 128), part)]
            slot = (my_step * KPARTS + k) * 8 + y_hi * 4 + z
            here = jnp.logical_and(i == 0, own == 1)

            @pl.when(here)
            def _():
                pltpu.make_async_copy(src, landed.at[slot], land_sem.at[my_step, k]).start()

            @pl.when(jnp.logical_not(here))
            def _():
                pltpu.make_async_remote_copy(
                    src_ref=src, dst_ref=landed.at[slot], send_sem=send_sem, recv_sem=land_sem.at[my_step, k],
                    device_id=device(to_x, to_y, to_z, core), device_id_type=MESH,
                ).start()

            return 0

        lax.fori_loop(0, 32 * KPARTS, one, 0)

    def block_ref(t, kk, ss, k):
        return panel.at[k, pl.ds(pl.multiple_of(t * STEP + kk * 2 * BLOCK + ss * BLOCK, 16), BLOCK), :]

    def forward(t, kk, k, to, sem):
        ref = block_ref(t, kk, s, k)
        return pltpu.make_async_remote_copy(
            src_ref=ref, dst_ref=ref, send_sem=sem, recv_sem=block_sem.at[t, kk * 2 + s, k],
            device_id=to, device_id_type=MESH,
        )

    def wait_block(t, kk, ss, k):
        ref = block_ref(t, kk, ss, k)
        pltpu.make_async_copy(ref, ref, block_sem.at[t, kk * 2 + ss, k]).wait()

    def take(t, k):
        base = (t * KPARTS + k) * 8
        eight = landed.at[pl.ds(base, 8)]
        pltpu.make_async_copy(eight, eight, land_sem.at[t, k]).wait()
        row0 = pl.multiple_of(t * STEP + kind * 2 * BLOCK + s * BLOCK, 16)
        width = min(part, 512)

        def repack(i, _):
            lanes = pl.ds(pl.multiple_of(i * width, width), width)
            for m in range(8):
                wide[pl.ds(m * ROWS, ROWS), :] = landed[base + m, :, lanes].astype(jnp.float32)
            panel[k, pl.ds(row0, BLOCK), lanes] = wide[...].astype(jnp.bfloat16)
            return 0

        lax.fori_loop(0, part // width, repack, 0)
        forward(t, kind, k, pair, pair_send.at[t, k]).start()
        forward(t, kind, k, sibling, sib_send.at[t, 0, k]).start()

    def relay(t, k):
        wait_block(t, 1 - kind, s, k)
        forward(t, 1 - kind, k, sibling, sib_send.at[t, 1, k]).start()

    def gather_sibling(t):
        def one(k, _):
            wait_block(t, kind, 1 - s, k)
            wait_block(t, 1 - kind, 1 - s, k)
            return 0

        lax.fori_loop(0, KPARTS, one, 0)

    def multiply(t):
        def tile(n, _):
            lanes = pl.ds(pl.multiple_of(n * 256, 256), 256)

            def add(k, total):
                return total + lax.dot_general(
                    panel[k, pl.ds(t * STEP, STEP), :],
                    integrals[lanes, pl.ds(pl.multiple_of(k * part, part), part)],
                    (((1,), (1,)), ((), ())),
                    preferred_element_type=jnp.float32,
                )

            total = lax.fori_loop(0, KPARTS, add, jnp.zeros((STEP, 256), jnp.float32))
            for kk in range(2):
                for r in range(2):
                    for u in range(2):
                        row = (kk * 2 + r) * BLOCK + u * PIECE
                        parts[t, 2 * r + u, pl.ds(kk * PIECE, PIECE), lanes] = total[row:row + PIECE]
            return 0

        lax.fori_loop(0, integrals.shape[0] // 256, tile, 0)

    def z_copy(t, d):
        return pltpu.make_async_remote_copy(
            src_ref=parts.at[t, (z + d) % 4], dst_ref=from_z.at[t, d - 1],
            send_sem=z_send.at[t, d - 1], recv_sem=z_recv.at[t, d - 1],
            device_id=device(x, y, (z + d) % 4, s), device_id_type=MESH,
        )

    def send_z(t):
        for d in (1, 3, 2):
            z_copy(t, d).start()

    u = z % 2

    def owner(t, kk):
        return 2 * ((kk + u) % 2) + t // 2, t % 2

    def xy_copy(t, kk):
        to_x, to_yhi = owner(t, kk)
        d = (x - to_x + 4) % 4 + 4 * ((y_hi + to_yhi) % 2)
        return d, pltpu.make_async_remote_copy(
            src_ref=reduced.at[t, pl.ds(kk * PIECE, PIECE)], dst_ref=from_xy.at[d],
            send_sem=xy_send.at[t, kk], recv_sem=xy_recv.at[d],
            device_id=device(to_x, to_yhi * 2 + y_lo, z, s), device_id_type=MESH,
        )

    def reduce_z(t):
        for d in range(1, 4):
            z_copy(t, d).wait_recv()
        reduced[t] = 0.5 * (parts[t, z] + from_z[t, 0] + from_z[t, 1] + from_z[t, 2])
        for kk in range(2):
            d, cp = xy_copy(t, kk)

            @pl.when(d != 0)
            def _():
                cp.start()

            @pl.when(d == 0)
            def _():
                from_xy[0] = reduced[t, pl.ds(kk * PIECE, PIECE)]

    @pl.when(s == 0)
    def _():
        send_all()

    for k in range(KPARTS):
        for t in (0, 1):
            take(t, k)

    @pl.when(s == 1)
    def _():
        send_all()

    for k in range(KPARTS):
        for t in (0, 1):
            relay(t, k)
    for t in (2, 3):
        for k in range(KPARTS):
            take(t, k)
    load.wait()
    for t in (0, 1):
        gather_sibling(t)
        multiply(t)
        send_z(t)
    for k in range(KPARTS):
        relay(2, k)
    reduce_z(0)
    gather_sibling(2)
    multiply(2)
    send_z(2)
    reduce_z(1)
    for k in range(KPARTS):
        relay(3, k)
    gather_sibling(3)
    multiply(3)
    send_z(3)
    reduce_z(2)
    reduce_z(3)

    total = from_xy[0]
    for d in range(1, 8):
        pltpu.make_async_copy(from_xy.at[d], from_xy.at[d], xy_recv.at[d]).wait()
        total = total + from_xy[d]
    out[...] = total

    many = 32 * KPARTS

    @pl.when(own == 1)
    def _():
        left = landed.at[pl.ds(0, many - KPARTS)]
        pltpu.make_async_copy(left, left, send_sem).wait()

    @pl.when(own == 0)
    def _():
        left = landed.at[pl.ds(0, many)]
        pltpu.make_async_copy(left, left, send_sem).wait()

    for t in range(STEPS):
        for k in range(KPARTS):
            forward(t, kind, k, pair, pair_send.at[t, k]).wait_send()
            forward(t, kind, k, sibling, sib_send.at[t, 0, k]).wait_send()
            forward(t, 1 - kind, k, sibling, sib_send.at[t, 1, k]).wait_send()
        for d in range(1, 4):
            z_copy(t, d).wait_send()
        for kk in range(2):
            d, cp = xy_copy(t, kk)

            @pl.when(d != 0)
            def _():
                cp.wait_send()


def per_device(amplitudes, integrals):
    ab, cols = integrals.shape
    part = cols // KPARTS
    return pl.pallas_call(
        kernel,
        out_shape=jax.ShapeDtypeStruct((PIECE, ab), jnp.float32),
        in_specs=[pl.BlockSpec(memory_space=pl.ANY)] * 2,
        out_specs=pl.BlockSpec(memory_space=pltpu.VMEM),
        scratch_shapes=[
            pltpu.VMEM((ab, cols), jnp.bfloat16),
            pltpu.VMEM((32 * KPARTS, ROWS, part), jnp.bfloat16),
            pltpu.VMEM((BLOCK, min(part, 512)), jnp.float32),
            pltpu.VMEM((KPARTS, STEPS * STEP, part), jnp.bfloat16),
            pltpu.VMEM((STEPS, 4, 2 * PIECE, ab), jnp.float32),
            pltpu.VMEM((STEPS, 3, 2 * PIECE, ab), jnp.float32),
            pltpu.VMEM((STEPS, 2 * PIECE, ab), jnp.float32),
            pltpu.VMEM((8, PIECE, ab), jnp.float32),
            pltpu.SemaphoreType.DMA,
            pltpu.SemaphoreType.DMA,
            pltpu.SemaphoreType.DMA((STEPS, KPARTS)),
            pltpu.SemaphoreType.DMA((STEPS, KPARTS)),
            pltpu.SemaphoreType.DMA((STEPS, 2, KPARTS)),
            pltpu.SemaphoreType.DMA((STEPS, 4, KPARTS)),
            pltpu.SemaphoreType.DMA((STEPS, 3)),
            pltpu.SemaphoreType.DMA((STEPS, 3)),
            pltpu.SemaphoreType.DMA((STEPS, 2)),
            pltpu.SemaphoreType.DMA((8,)),
        ],
        compiler_params=pltpu.CompilerParams(
            collective_id=0, has_side_effects=True, vmem_limit_bytes=60 * 2**20
        ),
        cost_estimate=pl.CostEstimate(
            flops=2 * STEPS * STEP * ab * cols, bytes_accessed=2 * ab * cols, transcendentals=0
        ),
        name="ladder",
    )(amplitudes, integrals)


def solution(mesh):
    return jax.shard_map(
        per_device,
        mesh=mesh,
        in_specs=(P(("grp", "col"), None), P("grp", "col")),
        out_specs=P("col", "grp"),
        check_vma=False,
    )
```

```python
import jax
import jax.numpy as jnp
from jax import lax
from jax.experimental import pallas as pl
from jax.experimental.pallas import tpu as pltpu
from jax.sharding import PartitionSpec as P

MESH = pl.DeviceIdType.MESH
ROWS = 6
BLOCK = 8 * ROWS
STEP = 4 * BLOCK
STEPS = 4
PIECE = 24
KPARTS = 8
MPARTS = 4
WIDE = 512
AHEAD = 3


def device(x, y, z, s):
    return ((y % 2) * 2 + s, (x * 2 + y // 2) * 4 + z)


def across(y):
    return (y + 3 + 2 * (y % 2)) % 4


def kernel(amp, integrals_hbm, out, integrals, landed, wide, panel, parts, from_z, reduced, from_x, summed, from_y,
           load_sem, send_sem, land_sem, pair_send, sib_send, block_sem, z_send, z_recv, x_send, x_recv, y_send, y_recv):
    g = lax.axis_index("grp")
    c = lax.axis_index("col")
    x, y, z, s = c // 8, (c // 4) % 2 * 2 + g // 2, c % 4, g % 2
    y_hi, y_lo = y // 2, y % 2
    kind = (y_lo + y_hi) % 2
    cols = integrals.shape[1]
    part = cols // KPARTS
    per = KPARTS // MPARTS
    tiles = integrals.shape[0] // WIDE
    core = x % 2
    own = jnp.where(s == core, 1, 0)
    pair = device(x, y + 1 - 2 * y_lo, z, s)
    sibling = device(x, y, z, 1 - s)

    load = pltpu.make_async_copy(integrals_hbm, integrals, load_sem)
    load.start()

    bar = pltpu.get_barrier_semaphore()

    def greet(i, _):
        src_x = 2 * (i % 2) + s
        src_y = jnp.where((i // 2) % 2 == 0, y, across(y))
        src_z = (i // 4) % 4
        src_s = i // 16
        other = jnp.logical_not((src_x == x) & (src_y == y) & (src_z == z) & (src_s == s))

        @pl.when(other)
        def _():
            pl.semaphore_signal(bar, inc=1, device_id=device(src_x, src_y, src_z, src_s), device_id_type=MESH)

        return 0

    lax.fori_loop(0, 32, greet, 0)
    pl.semaphore_signal(bar, inc=1, device_id=pair, device_id_type=MESH)
    pl.semaphore_signal(bar, inc=1, device_id=sibling, device_id_type=MESH)
    for d in range(1, 4):
        pl.semaphore_signal(bar, inc=1, device_id=device(x, y, (z + d) % 4, s), device_id_type=MESH)
        pl.semaphore_signal(bar, inc=1, device_id=device((x + d) % 4, y, z, s), device_id_type=MESH)
    pl.semaphore_signal(bar, inc=1, device_id=device(x, (y + 2) % 4, z, s), device_id_type=MESH)
    parts[...] = jnp.zeros_like(parts)
    pl.semaphore_wait(bar, 41 - own)

    my_step = s * 2 + x // 2

    def send_part(k):
        def one(i, _):
            j, m = i // 2, i % 2
            dx = j % 4
            dz = (j // 4 + j) % 4
            to_x = jnp.where(m == 0, x + dx, x - dx + 4) % 4
            to_z = jnp.where(m == 0, z + dz, z - dz + 4) % 4
            to_y = jnp.where(m == 0, y, across(y))
            to_col = (to_x * 2 + to_y // 2) * 4 + to_z
            src = amp.at[:, pl.ds(pl.multiple_of(to_col * cols + k * part, 128), part)]
            slot = (my_step * KPARTS + k) * 8 + y_hi * 4 + z
            here = jnp.logical_and(i == 0, own == 1)

            @pl.when(here)
            def _():
                pltpu.make_async_copy(src, landed.at[slot], land_sem.at[my_step, k]).start()

            @pl.when(jnp.logical_not(here))
            def _():
                pltpu.make_async_remote_copy(
                    src_ref=src, dst_ref=landed.at[slot], send_sem=send_sem, recv_sem=land_sem.at[my_step, k],
                    device_id=device(to_x, to_y, to_z, core), device_id_type=MESH,
                ).start()

            return 0

        lax.fori_loop(0, 32, one, 0)

    def send_parts(who, first, last):
        if first < last:
            @pl.when(s == who)
            def _():
                lax.fori_loop(first, last, lambda k, _: (send_part(k), 0)[1], 0)

    def block_ref(t, kk, ss, k):
        rows = pl.ds(pl.multiple_of(t * STEP + kk * 2 * BLOCK + ss * BLOCK, 16), BLOCK)
        return panel.at[k // per, rows, pl.ds(pl.multiple_of(k % per * part, 128), part)]

    def forward(t, kk, k, to, sem):
        ref = block_ref(t, kk, s, k)
        return pltpu.make_async_remote_copy(
            src_ref=ref, dst_ref=ref, send_sem=sem, recv_sem=block_sem.at[t, kk * 2 + s, k],
            device_id=to, device_id_type=MESH,
        )

    def wait_block(t, kk, ss, k):
        ref = block_ref(t, kk, ss, k)
        pltpu.make_async_copy(ref, ref, block_sem.at[t, kk * 2 + ss, k]).wait()

    def take(t, k):
        base = (t * KPARTS + k) * 8
        eight = landed.at[pl.ds(base, 8)]
        pltpu.make_async_copy(eight, eight, land_sem.at[t, k]).wait()
        row0 = pl.multiple_of(t * STEP + kind * 2 * BLOCK + s * BLOCK, 16)
        width = min(part, 512)

        def repack(i, _):
            lanes = pl.ds(pl.multiple_of(i * width, width), width)
            to = pl.ds(pl.multiple_of(k % per * part + i * width, width), width)
            for m in range(8):
                wide[pl.ds(m * ROWS, ROWS), :] = landed[base + m, :, lanes].astype(jnp.float32)
            panel[k // per, pl.ds(row0, BLOCK), to] = wide[...].astype(jnp.bfloat16)
            return 0

        lax.fori_loop(0, part // width, repack, 0)
        forward(t, kind, k, pair, pair_send.at[t, k]).start()
        forward(t, kind, k, sibling, sib_send.at[t, 0, k]).start()

    def relay(t, k):
        wait_block(t, 1 - kind, s, k)
        forward(t, 1 - kind, k, sibling, sib_send.at[t, 1, k]).start()

    def wait_sibling(t, k):
        wait_block(t, kind, 1 - s, k)
        wait_block(t, 1 - kind, 1 - s, k)

    def z_copy(t, n, d):
        return pltpu.make_async_remote_copy(
            src_ref=parts.at[t, (z + d) % 4, n], dst_ref=from_z.at[t, d - 1, n],
            send_sem=z_send.at[t, d - 1, n], recv_sem=z_recv.at[t, d - 1, n],
            device_id=device(x, y, (z + d) % 4, s), device_id_type=MESH,
        )

    def multiply(t, km):
        width = per * part

        def tile(n, _):
            lanes = pl.ds(pl.multiple_of(n * WIDE, WIDE), WIDE)
            total = lax.dot_general(
                panel[km, pl.ds(pl.multiple_of(t * STEP, 16), STEP), :],
                integrals[lanes, pl.ds(pl.multiple_of(km * width, width), width)],
                (((1,), (1,)), ((), ())),
                preferred_element_type=jnp.float32,
            )
            for kk in range(2):
                for r in range(2):
                    for u in range(2):
                        row = (kk * 2 + r) * BLOCK + u * PIECE
                        parts[t, 2 * r + u, n, pl.ds(kk * PIECE, PIECE), :] += total[row:row + PIECE]

            @pl.when(km == MPARTS - 1)
            def _():
                for d in (2, 1, 3):
                    z_copy(t, n, d).start()

            return 0

        lax.fori_loop(0, tiles, tile, 0)

    def multiply_steps(first, last, km):
        lax.fori_loop(first, last, lambda t, _: (multiply(t, km), 0)[1], 0)

    u = z % 2

    def x_copy(t, n, kk):
        to_x = 2 * ((kk + u) % 2) + t // 2
        d = (to_x - x + 4) % 4
        place = jnp.maximum(d, 1) - 1
        return d, pltpu.make_async_remote_copy(
            src_ref=reduced.at[t, n, pl.ds(kk * PIECE, PIECE)], dst_ref=from_x.at[t % 2, place, n],
            send_sem=x_send.at[t, n, kk], recv_sem=x_recv.at[t % 2, place, n],
            device_id=device(to_x, y, z, s), device_id_type=MESH,
        )

    def y_copy(n):
        return pltpu.make_async_remote_copy(
            src_ref=summed.at[1, n], dst_ref=from_y.at[n], send_sem=y_send.at[n], recv_sem=y_recv.at[n],
            device_id=device(x, (y + 2) % 4, z, s), device_id_type=MESH,
        )

    def reduce_z(t):
        def one(n, _):
            for d in range(1, 4):
                z_copy(t, n, d).wait_recv()
            reduced[t, n] = 0.5 * (parts[t, z, n] + from_z[t, 0, n] + from_z[t, 1, n] + from_z[t, 2, n])
            for kk in range(2):
                d, cp = x_copy(t, n, kk)
                pl.when(d != 0)(cp.start)
            return 0

        lax.fori_loop(0, tiles, one, 0)

    def reduce_x(t):
        @pl.when(x % 2 == t // 2)
        def _():
            kk = (x // 2 + u) % 2
            mine = jnp.where(y_hi == t % 2, 0, 1)

            def one(n, _):
                for d in range(3):
                    ref = from_x.at[t % 2, d, n]
                    pltpu.make_async_copy(ref, ref, x_recv.at[t % 2, d, n]).wait()
                rows = pl.ds(pl.multiple_of(kk * PIECE, 8), PIECE)
                summed[mine, n] = reduced[t, n, rows, :] + from_x[t % 2, 0, n] + from_x[t % 2, 1, n] + from_x[t % 2, 2, n]
                pl.when(mine == 1)(y_copy(n).start)
                return 0

            lax.fori_loop(0, tiles, one, 0)

    send_parts(0, 0, AHEAD)
    for k in range(KPARTS):
        take(0, k)
        take(1, k)
        send_parts(0, k + AHEAD, min(k + AHEAD + 1, KPARTS))
        if k >= 3:
            send_parts(1, k - 3, k - 2)
        if k >= 2:
            relay(0, k - 2)
            relay(1, k - 2)
        if k == 0:
            load.wait()
        if k >= 4 and k % per == 0:
            km = (k - 4) // per
            for kt in range(km * per, km * per + per):
                wait_sibling(0, kt)
                wait_sibling(1, kt)
            multiply_steps(0, 2, km)
    send_parts(1, KPARTS - 3, KPARTS)
    for k in range(KPARTS):
        take(2, k)
        if k < 2:
            relay(0, KPARTS - 2 + k)
            relay(1, KPARTS - 2 + k)
        if k in (2, 4):
            km = MPARTS - 2 + (k - 2) // 2
            for kt in range(km * per, km * per + per):
                wait_sibling(0, kt)
                wait_sibling(1, kt)
            multiply_steps(0, 2, km)

    def third(km, _):
        def one(i, _):
            take(3, km * per + i)
            relay(2, km * per + i)
            return 0

        lax.fori_loop(0, per, one, 0)
        lax.fori_loop(0, per, lambda i, _: (wait_sibling(2, km * per + i), 0)[1], 0)
        multiply(2, km)

        @pl.when(km < 2)
        def _():
            reduce_z(km)

        return 0

    lax.fori_loop(0, MPARTS, third, 0)

    def fourth(km, _):
        lax.fori_loop(0, per, lambda i, _: (relay(3, km * per + i), 0)[1], 0)
        lax.fori_loop(0, per, lambda i, _: (wait_sibling(3, km * per + i), 0)[1], 0)
        multiply(3, km)

        @pl.when(km < 2)
        def _():
            reduce_x(km)

        @pl.when(km == 2)
        def _():
            reduce_z(2)

        return 0

    lax.fori_loop(0, MPARTS, fourth, 0)
    reduce_x(2)
    reduce_z(3)
    reduce_x(3)

    for n in range(tiles):
        y_copy(n).wait_recv()
        out[:, n * WIDE:n * WIDE + WIDE] = summed[0, n] + from_y[n]

    many = 32 * KPARTS

    @pl.when(own == 1)
    def _():
        left = landed.at[pl.ds(0, many - KPARTS)]
        pltpu.make_async_copy(left, left, send_sem).wait()

    @pl.when(own == 0)
    def _():
        left = landed.at[pl.ds(0, many)]
        pltpu.make_async_copy(left, left, send_sem).wait()

    for t in range(STEPS):
        for k in range(KPARTS):
            forward(t, kind, k, pair, pair_send.at[t, k]).wait_send()
            forward(t, kind, k, sibling, sib_send.at[t, 0, k]).wait_send()
            forward(t, 1 - kind, k, sibling, sib_send.at[t, 1, k]).wait_send()
        for n in range(tiles):
            for d in range(1, 4):
                z_copy(t, n, d).wait_send()
            for kk in range(2):
                d, cp = x_copy(t, n, kk)
                pl.when(d != 0)(cp.wait_send)
    for n in range(tiles):
        y_copy(n).wait_send()


def per_device(amplitudes, integrals):
    ab, cols = integrals.shape
    part = cols // KPARTS
    tiles = ab // WIDE
    return pl.pallas_call(
        kernel,
        out_shape=jax.ShapeDtypeStruct((PIECE, ab), jnp.float32),
        in_specs=[pl.BlockSpec(memory_space=pl.ANY)] * 2,
        out_specs=pl.BlockSpec(memory_space=pltpu.VMEM),
        scratch_shapes=[
            pltpu.VMEM((ab, cols), jnp.bfloat16),
            pltpu.VMEM((32 * KPARTS, ROWS, part), jnp.bfloat16),
            pltpu.VMEM((BLOCK, min(part, 512)), jnp.float32),
            pltpu.VMEM((MPARTS, STEPS * STEP, cols // MPARTS), jnp.bfloat16),
            pltpu.VMEM((STEPS, 4, tiles, 2 * PIECE, WIDE), jnp.float32),
            pltpu.VMEM((STEPS, 3, tiles, 2 * PIECE, WIDE), jnp.float32),
            pltpu.VMEM((STEPS, tiles, 2 * PIECE, WIDE), jnp.float32),
            pltpu.VMEM((2, 3, tiles, PIECE, WIDE), jnp.float32),
            pltpu.VMEM((2, tiles, PIECE, WIDE), jnp.float32),
            pltpu.VMEM((tiles, PIECE, WIDE), jnp.float32),
            pltpu.SemaphoreType.DMA,
            pltpu.SemaphoreType.DMA,
            pltpu.SemaphoreType.DMA((STEPS, KPARTS)),
            pltpu.SemaphoreType.DMA((STEPS, KPARTS)),
            pltpu.SemaphoreType.DMA((STEPS, 2, KPARTS)),
            pltpu.SemaphoreType.DMA((STEPS, 4, KPARTS)),
            pltpu.SemaphoreType.DMA((STEPS, 3, tiles)),
            pltpu.SemaphoreType.DMA((STEPS, 3, tiles)),
            pltpu.SemaphoreType.DMA((STEPS, tiles, 2)),
            pltpu.SemaphoreType.DMA((2, 3, tiles)),
            pltpu.SemaphoreType.DMA((tiles,)),
            pltpu.SemaphoreType.DMA((tiles,)),
        ],
        compiler_params=pltpu.CompilerParams(
            collective_id=0, has_side_effects=True, vmem_limit_bytes=60 * 2**20
        ),
        cost_estimate=pl.CostEstimate(
            flops=2 * STEPS * STEP * ab * cols, bytes_accessed=2 * ab * cols, transcendentals=0
        ),
        name="ladder",
    )(amplitudes, integrals)


def solution(mesh):
    return jax.shard_map(
        per_device,
        mesh=mesh,
        in_specs=(P(("grp", "col"), None), P("grp", "col")),
        out_specs=P("col", "grp"),
        check_vma=False,
    )
```

```python
import jax
import jax.numpy as jnp
from jax import lax
from jax.experimental import pallas as pl
from jax.experimental.pallas import tpu as pltpu
from jax.sharding import PartitionSpec as P

MESH = pl.DeviceIdType.MESH
ROWS = 6
BLOCK = 8 * ROWS
STEP = 4 * BLOCK
STEPS = 4
PIECE = 24
KPARTS = 8
MPARTS = 4
HALF = 512
FINE = 128
AHEAD = 3


def device(x, y, z, s):
    return ((y % 2) * 2 + s, (x * 2 + y // 2) * 4 + z)


def across(y):
    return (y + 3 + 2 * (y % 2)) % 4


def kernel(amp, integrals_hbm, out, integrals, landed, wide, panel, total, parts, from_z, reduced, from_x, summed, from_y,
           parts_b, from_xb, reduced_b, from_zb, summed_b, from_xyb,
           load_sem, send_sem, land_sem, pair_send, sib_send, block_sem, z_send, z_recv, x_send, x_recv, y_send, y_recv,
           xb_send, xb_recv, zb_send, zb_recv, xyb_send, xyb_recv):
    g = lax.axis_index("grp")
    c = lax.axis_index("col")
    x, y, z, s = c // 8, (c // 4) % 2 * 2 + g // 2, c % 4, g % 2
    y_hi, y_lo = y // 2, y % 2
    kind = (y_lo + y_hi) % 2
    cols = integrals.shape[1]
    part = cols // KPARTS
    per = KPARTS // MPARTS
    core = x % 2
    own = jnp.where(s == core, 1, 0)
    pair = device(x, y + 1 - 2 * y_lo, z, s)
    sibling = device(x, y, z, 1 - s)

    load = pltpu.make_async_copy(integrals_hbm, integrals, load_sem)
    load.start()

    bar = pltpu.get_barrier_semaphore()

    def greet(i, _):
        src_x = 2 * (i % 2) + s
        src_y = jnp.where((i // 2) % 2 == 0, y, across(y))
        src_z = (i // 4) % 4
        src_s = i // 16
        other = jnp.logical_not((src_x == x) & (src_y == y) & (src_z == z) & (src_s == s))

        @pl.when(other)
        def _():
            pl.semaphore_signal(bar, inc=1, device_id=device(src_x, src_y, src_z, src_s), device_id_type=MESH)

        return 0

    lax.fori_loop(0, 32, greet, 0)
    pl.semaphore_signal(bar, inc=1, device_id=pair, device_id_type=MESH)
    pl.semaphore_signal(bar, inc=1, device_id=sibling, device_id_type=MESH)
    for d in range(1, 4):
        pl.semaphore_signal(bar, inc=1, device_id=device(x, y, (z + d) % 4, s), device_id_type=MESH)
        pl.semaphore_signal(bar, inc=1, device_id=device((x + d) % 4, y, z, s), device_id_type=MESH)
    pl.semaphore_signal(bar, inc=1, device_id=device(x, (y + 2) % 4, z, s), device_id_type=MESH)
    for d in range(1, 4):
        pl.semaphore_signal(bar, inc=1, device_id=device((x + d) % 4, (y + 2) % 4, z, s), device_id_type=MESH)
    parts[...] = jnp.zeros_like(parts)
    parts_b[...] = jnp.zeros_like(parts_b)
    pl.semaphore_wait(bar, 44 - own)

    my_step = s * 2 + x // 2

    def send_part(k):
        def one(i, _):
            j, m = i // 2, i % 2
            dx = j % 4
            dz = (j // 4 + j) % 4
            to_x = jnp.where(m == 0, x + dx, x - dx + 4) % 4
            to_z = jnp.where(m == 0, z + dz, z - dz + 4) % 4
            to_y = jnp.where(m == 0, y, across(y))
            to_col = (to_x * 2 + to_y // 2) * 4 + to_z
            src = amp.at[:, pl.ds(pl.multiple_of(to_col * cols + k * part, 128), part)]
            slot = (my_step * KPARTS + k) * 8 + y_hi * 4 + z
            here = jnp.logical_and(i == 0, own == 1)

            @pl.when(here)
            def _():
                pltpu.make_async_copy(src, landed.at[slot], land_sem.at[my_step, k]).start()

            @pl.when(jnp.logical_not(here))
            def _():
                pltpu.make_async_remote_copy(
                    src_ref=src, dst_ref=landed.at[slot], send_sem=send_sem, recv_sem=land_sem.at[my_step, k],
                    device_id=device(to_x, to_y, to_z, core), device_id_type=MESH,
                ).start()

            return 0

        lax.fori_loop(0, 32, one, 0)

    def send_parts(who, first, last):
        if first < last:
            @pl.when(s == who)
            def _():
                lax.fori_loop(first, last, lambda k, _: (send_part(k), 0)[1], 0)

    def block_ref(t, kk, ss, k):
        rows = pl.ds(pl.multiple_of(t * STEP + kk * 2 * BLOCK + ss * BLOCK, 16), BLOCK)
        return panel.at[k // per, rows, pl.ds(pl.multiple_of(k % per * part, 128), part)]

    def forward(t, kk, k, to, sem):
        ref = block_ref(t, kk, s, k)
        return pltpu.make_async_remote_copy(
            src_ref=ref, dst_ref=ref, send_sem=sem, recv_sem=block_sem.at[t, kk * 2 + s, k],
            device_id=to, device_id_type=MESH,
        )

    def wait_block(t, kk, ss, k):
        ref = block_ref(t, kk, ss, k)
        pltpu.make_async_copy(ref, ref, block_sem.at[t, kk * 2 + ss, k]).wait()

    def take(t, k):
        base = (t * KPARTS + k) * 8
        eight = landed.at[pl.ds(base, 8)]
        pltpu.make_async_copy(eight, eight, land_sem.at[t, k]).wait()
        row0 = pl.multiple_of(t * STEP + kind * 2 * BLOCK + s * BLOCK, 16)
        width = min(part, 512)

        def repack(i, _):
            lanes = pl.ds(pl.multiple_of(i * width, width), width)
            to = pl.ds(pl.multiple_of(k % per * part + i * width, width), width)
            for m in range(8):
                wide[pl.ds(m * ROWS, ROWS), :] = landed[base + m, :, lanes].astype(jnp.float32)
            panel[k // per, pl.ds(row0, BLOCK), to] = wide[...].astype(jnp.bfloat16)
            return 0

        lax.fori_loop(0, part // width, repack, 0)
        forward(t, kind, k, pair, pair_send.at[t, k]).start()
        forward(t, kind, k, sibling, sib_send.at[t, 0, k]).start()

    def relay(t, k):
        wait_block(t, 1 - kind, s, k)
        forward(t, 1 - kind, k, sibling, sib_send.at[t, 1, k]).start()

    def wait_sibling(t, k):
        wait_block(t, kind, 1 - s, k)
        wait_block(t, 1 - kind, 1 - s, k)

    def z_copy(t, d):
        return pltpu.make_async_remote_copy(
            src_ref=parts.at[t, (z + d) % 4], dst_ref=from_z.at[t, d - 1],
            send_sem=z_send.at[t, d - 1], recv_sem=z_recv.at[t, d - 1],
            device_id=device(x, y, (z + d) % 4, s), device_id_type=MESH,
        )

    def xb_copy(t, d):
        return pltpu.make_async_remote_copy(
            src_ref=parts_b.at[t, (x + d) % 4], dst_ref=from_xb.at[t, d - 1],
            send_sem=xb_send.at[t, d - 1], recv_sem=xb_recv.at[t, d - 1],
            device_id=device((x + d) % 4, y, z, s), device_id_type=MESH,
        )

    def multiply(t, km):
        width = per * part
        last = km == MPARTS - 1

        def half(n, _):
            total[...] = lax.dot_general(
                panel[km, pl.ds(pl.multiple_of(t * STEP, 16), STEP), :],
                integrals[pl.ds(pl.multiple_of(n * HALF, HALF), HALF), pl.ds(pl.multiple_of(km * width, width), width)],
                (((1,), (1,)), ((), ())),
                preferred_element_type=jnp.float32,
            )

            @pl.when(n == 0)
            def _():
                for kk in range(2):
                    for r in range(2):
                        for u in range(2):
                            row = (kk * 2 + r) * BLOCK + u * PIECE
                            parts[t, 2 * r + u, pl.ds(kk * PIECE, PIECE), :] += total[row:row + PIECE, :]

                @pl.when(last)
                def _():
                    for d in (2, 1, 3):
                        z_copy(t, d).start()

            @pl.when(n == 1)
            def _():
                for q in range(4):
                    for kk in range(2):
                        for r in range(2):
                            for u in range(2):
                                row = (kk * 2 + r) * BLOCK + u * PIECE
                                parts_b[t, q, 2 * r + u, pl.ds(kk * PIECE, PIECE), :] += total[
                                    row:row + PIECE, q * FINE:q * FINE + FINE]

                @pl.when(last)
                def _():
                    for d in (2, 1, 3):
                        xb_copy(t, d).start()

            return 0

        lax.fori_loop(0, 2, half, 0)

    def multiply_steps(first, last, km):
        lax.fori_loop(first, last, lambda t, _: (multiply(t, km), 0)[1], 0)

    u = z % 2

    def owner_x(t, kk):
        return 2 * ((kk + u) % 2) + t // 2

    def x_copy(t, kk):
        d = (owner_x(t, kk) - x + 4) % 4
        place = jnp.maximum(d, 1) - 1
        return d, pltpu.make_async_remote_copy(
            src_ref=reduced.at[t, pl.ds(kk * PIECE, PIECE)], dst_ref=from_x.at[t % 2, place],
            send_sem=x_send.at[t, kk], recv_sem=x_recv.at[t % 2, place],
            device_id=device(owner_x(t, kk), y, z, s), device_id_type=MESH,
        )

    def y_copy():
        return pltpu.make_async_remote_copy(
            src_ref=summed.at[1], dst_ref=from_y, send_sem=y_send, recv_sem=y_recv,
            device_id=device(x, (y + 2) % 4, z, s), device_id_type=MESH,
        )

    def reduce_z(t):
        for d in range(1, 4):
            z_copy(t, d).wait_recv()
        reduced[t] = 0.5 * (parts[t, z] + from_z[t, 0] + from_z[t, 1] + from_z[t, 2])
        for kk in range(2):
            d, cp = x_copy(t, kk)
            pl.when(d != 0)(cp.start)

    def reduce_x(t):
        @pl.when(x % 2 == t // 2)
        def _():
            kk = (x // 2 + u) % 2
            mine = jnp.where(y_hi == t % 2, 0, 1)
            for d in range(3):
                ref = from_x.at[t % 2, d]
                pltpu.make_async_copy(ref, ref, x_recv.at[t % 2, d]).wait()
            rows = pl.ds(pl.multiple_of(kk * PIECE, 8), PIECE)
            summed[mine] = reduced[t, rows, :] + from_x[t % 2, 0] + from_x[t % 2, 1] + from_x[t % 2, 2]
            pl.when(mine == 1)(y_copy().start)

    def zb_copy(t, d):
        return pltpu.make_async_remote_copy(
            src_ref=reduced_b.at[t, (z + d) % 4], dst_ref=from_zb.at[t, d - 1],
            send_sem=zb_send.at[t, d - 1], recv_sem=zb_recv.at[t, d - 1],
            device_id=device(x, y, (z + d) % 4, s), device_id_type=MESH,
        )

    def reduce_xb(t):
        for d in range(1, 4):
            xb_copy(t, d).wait_recv()
        reduced_b[t] = 0.5 * (parts_b[t, x] + from_xb[t, 0] + from_xb[t, 1] + from_xb[t, 2])
        for d in (2, 1, 3):
            zb_copy(t, d).start()

    sender = x * 2 + y_hi

    def xyb_copy(t, kk):
        to_x = owner_x(t, kk)
        here = (to_x == x) & (y_hi == t % 2)
        return here, pltpu.make_async_remote_copy(
            src_ref=summed_b.at[t, pl.ds(kk * PIECE, PIECE)], dst_ref=from_xyb.at[sender],
            send_sem=xyb_send.at[t, kk], recv_sem=xyb_recv.at[sender],
            device_id=device(to_x, (t % 2) * 2 + y_lo, z, s), device_id_type=MESH,
        )

    def reduce_zb(t):
        for d in range(1, 4):
            zb_copy(t, d).wait_recv()
        summed_b[t] = reduced_b[t, z] + from_zb[t, 0] + from_zb[t, 1] + from_zb[t, 2]
        for kk in range(2):
            here, cp = xyb_copy(t, kk)
            pl.when(jnp.logical_not(here))(cp.start)

            @pl.when(here)
            def _():
                from_xyb[sender] = summed_b[t, pl.ds(kk * PIECE, PIECE), :]

    def end_sends(t):
        def one(k, _):
            forward(t, kind, k, pair, pair_send.at[t, k]).wait_send()
            forward(t, kind, k, sibling, sib_send.at[t, 0, k]).wait_send()
            forward(t, 1 - kind, k, sibling, sib_send.at[t, 1, k]).wait_send()
            return 0

        lax.fori_loop(0, KPARTS, one, 0)

    def end_sums(t):
        for d in range(1, 4):
            z_copy(t, d).wait_send()
            xb_copy(t, d).wait_send()
            zb_copy(t, d).wait_send()
        for kk in range(2):
            d, cp = x_copy(t, kk)
            pl.when(d != 0)(cp.wait_send)
            here, cp = xyb_copy(t, kk)
            pl.when(jnp.logical_not(here))(cp.wait_send)

    send_parts(0, 0, AHEAD)
    for k in range(KPARTS):
        take(0, k)
        take(1, k)
        send_parts(0, k + AHEAD, min(k + AHEAD + 1, KPARTS))
        if k >= 3:
            send_parts(1, k - 3, k - 2)
        if k >= 2:
            relay(0, k - 2)
            relay(1, k - 2)
        if k == 0:
            load.wait()
        if k >= 4 and k % per == 0:
            km = (k - 4) // per
            for kt in range(km * per, km * per + per):
                wait_sibling(0, kt)
                wait_sibling(1, kt)
            multiply_steps(0, 2, km)
    send_parts(1, KPARTS - 3, KPARTS)
    for k in range(KPARTS):
        take(2, k)
        if k < 2:
            relay(0, KPARTS - 2 + k)
            relay(1, KPARTS - 2 + k)
        if k in (2, 4):
            km = MPARTS - 2 + (k - 2) // 2
            for kt in range(km * per, km * per + per):
                wait_sibling(0, kt)
                wait_sibling(1, kt)
            multiply_steps(0, 2, km)

    def third(km, _):
        def one(i, _):
            take(3, km * per + i)
            relay(2, km * per + i)
            return 0

        lax.fori_loop(0, per, one, 0)
        lax.fori_loop(0, per, lambda i, _: (wait_sibling(2, km * per + i), 0)[1], 0)
        multiply(2, km)

        @pl.when(km < 2)
        def _():
            reduce_z(km)
            reduce_xb(km)

        @pl.when(km >= 2)
        def _():
            reduce_x(km - 2)
            reduce_zb(km - 2)

        return 0

    lax.fori_loop(0, MPARTS, third, 0)

    def fourth(km, _):
        lax.fori_loop(0, per, lambda i, _: (relay(3, km * per + i), 0)[1], 0)
        lax.fori_loop(0, per, lambda i, _: (wait_sibling(3, km * per + i), 0)[1], 0)
        multiply(3, km)

        @pl.when(km < 2)
        def _():
            end_sends(km)
            end_sums(km)

        @pl.when(km == 1)
        def _():
            reduce_z(2)
            reduce_xb(2)

        @pl.when(km == 2)
        def _():
            reduce_x(2)
            reduce_zb(2)
            end_sends(2)

        return 0

    lax.fori_loop(0, MPARTS, fourth, 0)
    reduce_z(3)
    reduce_xb(3)
    reduce_x(3)
    reduce_zb(3)

    y_copy().wait_recv()
    out[:, :HALF] = summed[0] + from_y[...]
    for q in range(4):
        for h in range(2):
            def arrive():
                ref = from_xyb.at[q * 2 + h]
                pltpu.make_async_copy(ref, ref, xyb_recv.at[q * 2 + h]).wait()

            pl.when(sender != q * 2 + h)(arrive)
        out[:, HALF + q * FINE:HALF + q * FINE + FINE] = from_xyb[q * 2] + from_xyb[q * 2 + 1]

    many = 32 * KPARTS

    @pl.when(own == 1)
    def _():
        left = landed.at[pl.ds(0, many - KPARTS)]
        pltpu.make_async_copy(left, left, send_sem).wait()

    @pl.when(own == 0)
    def _():
        left = landed.at[pl.ds(0, many)]
        pltpu.make_async_copy(left, left, send_sem).wait()

    end_sends(3)
    end_sums(2)
    end_sums(3)
    y_copy().wait_send()


def per_device(amplitudes, integrals):
    ab, cols = integrals.shape
    part = cols // KPARTS
    return pl.pallas_call(
        kernel,
        out_shape=jax.ShapeDtypeStruct((PIECE, ab), jnp.float32),
        in_specs=[pl.BlockSpec(memory_space=pl.ANY)] * 2,
        out_specs=pl.BlockSpec(memory_space=pltpu.VMEM),
        scratch_shapes=[
            pltpu.VMEM((ab, cols), jnp.bfloat16),
            pltpu.VMEM((32 * KPARTS, ROWS, part), jnp.bfloat16),
            pltpu.VMEM((BLOCK, min(part, 512)), jnp.float32),
            pltpu.VMEM((MPARTS, STEPS * STEP, cols // MPARTS), jnp.bfloat16),
            pltpu.VMEM((STEP, HALF), jnp.float32),
            pltpu.VMEM((STEPS, 4, 2 * PIECE, HALF), jnp.float32),
            pltpu.VMEM((STEPS, 3, 2 * PIECE, HALF), jnp.float32),
            pltpu.VMEM((STEPS, 2 * PIECE, HALF), jnp.float32),
            pltpu.VMEM((2, 3, PIECE, HALF), jnp.float32),
            pltpu.VMEM((2, PIECE, HALF), jnp.float32),
            pltpu.VMEM((PIECE, HALF), jnp.float32),
            pltpu.VMEM((STEPS, 4, 4, 2 * PIECE, FINE), jnp.float32),
            pltpu.VMEM((STEPS, 3, 4, 2 * PIECE, FINE), jnp.float32),
            pltpu.VMEM((STEPS, 4, 2 * PIECE, FINE), jnp.float32),
            pltpu.VMEM((STEPS, 3, 2 * PIECE, FINE), jnp.float32),
            pltpu.VMEM((STEPS, 2 * PIECE, FINE), jnp.float32),
            pltpu.VMEM((8, PIECE, FINE), jnp.float32),
            pltpu.SemaphoreType.DMA,
            pltpu.SemaphoreType.DMA,
            pltpu.SemaphoreType.DMA((STEPS, KPARTS)),
            pltpu.SemaphoreType.DMA((STEPS, KPARTS)),
            pltpu.SemaphoreType.DMA((STEPS, 2, KPARTS)),
            pltpu.SemaphoreType.DMA((STEPS, 4, KPARTS)),
            pltpu.SemaphoreType.DMA((STEPS, 3)),
            pltpu.SemaphoreType.DMA((STEPS, 3)),
            pltpu.SemaphoreType.DMA((STEPS, 2)),
            pltpu.SemaphoreType.DMA((2, 3)),
            pltpu.SemaphoreType.DMA,
            pltpu.SemaphoreType.DMA,
            pltpu.SemaphoreType.DMA((STEPS, 3)),
            pltpu.SemaphoreType.DMA((STEPS, 3)),
            pltpu.SemaphoreType.DMA((STEPS, 3)),
            pltpu.SemaphoreType.DMA((STEPS, 3)),
            pltpu.SemaphoreType.DMA((STEPS, 2)),
            pltpu.SemaphoreType.DMA((8,)),
        ],
        compiler_params=pltpu.CompilerParams(
            collective_id=0, has_side_effects=True, vmem_limit_bytes=60 * 2**20
        ),
        cost_estimate=pl.CostEstimate(
            flops=2 * STEPS * STEP * ab * cols, bytes_accessed=2 * ab * cols, transcendentals=0
        ),
        name="ladder",
    )(amplitudes, integrals)


def solution(mesh):
    return jax.shard_map(
        per_device,
        mesh=mesh,
        in_specs=(P(("grp", "col"), None), P("grp", "col")),
        out_specs=P("col", "grp"),
        check_vma=False,
    )
```

```python
import jax
import jax.numpy as jnp
from jax import lax
from jax.experimental import pallas as pl
from jax.experimental.pallas import tpu as pltpu
from jax.sharding import PartitionSpec as P

MESH = pl.DeviceIdType.MESH
ROWS = 6
BLOCK = 8 * ROWS
STEP = 4 * BLOCK
STEPS = 4
PIECE = 24
KPARTS = 8
MPARTS = 4
HALF = 512
FINE = 128
AHEAD = 3
GATE = 3
LAG = 2


def device(x, y, z, s):
    return ((y % 2) * 2 + s, (x * 2 + y // 2) * 4 + z)


def across(y):
    return (y + 3 + 2 * (y % 2)) % 4


def kernel(amp, integrals_hbm, out, slabs, integrals, landed, wide, panel, total, parts, from_z, reduced, from_x, summed, from_y,
           parts_b, from_xb, reduced_b, from_zb, summed_b, from_xyb,
           load_sem, send_sem, land_sem, pair_send, sib_send, block_sem, z_send, z_recv, x_send, x_recv, y_send, y_recv,
           xb_send, xb_recv, zb_send, zb_recv, xyb_send, xyb_recv):
    g = lax.axis_index("grp")
    c = lax.axis_index("col")
    x, y, z, s = c // 8, (c // 4) % 2 * 2 + g // 2, c % 4, g % 2
    y_hi, y_lo = y // 2, y % 2
    kind = (y_lo + y_hi) % 2
    cols = integrals.shape[0]
    part = cols // KPARTS
    per = KPARTS // MPARTS
    core = x % 2
    own = jnp.where(s == core, 1, 0)
    pair = device(x, y + 1 - 2 * y_lo, z, s)
    sibling = device(x, y, z, 1 - s)

    bar = pltpu.get_barrier_semaphore()

    across_lo, across_hi = 1 - y_lo, 1 - y_hi

    def hello(grp, col):
        pl.semaphore_signal(bar, inc=1, device_id=(grp, col), device_id_type=MESH)

    start_x = x + 1 - own

    def greet(i, _):
        src_x = lax.rem(start_x + 2 * lax.div(i, 4), 4)
        src_z = lax.rem(z + lax.rem(i, 4), 4)
        for src_s in range(2):
            hello(across_lo * 2 + src_s, src_x * 8 + across_hi * 4 + src_z)
            hello(y_lo * 2 + src_s, src_x * 8 + y_hi * 4 + src_z)
        return 0

    lax.fori_loop(1, 8, greet, 0)
    first_x = lax.rem(start_x, 4)
    for src_s in range(2):
        hello(across_lo * 2 + src_s, first_x * 8 + across_hi * 4 + z)
    hello(y_lo * 2 + 1 - s, first_x * 8 + y_hi * 4 + z)

    @pl.when(own == 0)
    def _():
        hello(y_lo * 2 + s, first_x * 8 + y_hi * 4 + z)

    hello(across_lo * 2 + s, c)
    hello(y_lo * 2 + 1 - s, c)
    for d in range(1, 4):
        hello(g, c - z + lax.rem(z + d, 4))
        hello(g, lax.rem(x + d, 4) * 8 + y_hi * 4 + z)
        hello(g, lax.rem(x + d, 4) * 8 + across_hi * 4 + z)
    hello(g, x * 8 + across_hi * 4 + z)
    slab = slabs.shape[1]
    n_slabs = integrals_hbm.shape[0] // slab

    def slab_copy(i):
        rows = pl.ds(pl.multiple_of(i * slab, slab), slab)
        return pltpu.make_async_copy(integrals_hbm.at[rows], slabs.at[i % 2], load_sem.at[i % 2])

    def turn_slab(i):
        slab_copy(i).wait()
        width = 1024

        def one(n, _):
            lanes = pl.ds(pl.multiple_of(n * width, width), width)
            integrals[lanes, pl.ds(i * slab, slab)] = slabs[i % 2, :, lanes].T
            return 0

        lax.fori_loop(0, cols // width, one, 0)
        if i + 2 < n_slabs:
            slab_copy(i + 2).start()

    parts[...] = jnp.zeros_like(parts)
    parts_b[...] = jnp.zeros_like(parts_b)
    pl.semaphore_wait(bar, 44 - own)

    my_step = s * 2 + x // 2

    mine_slot = my_step * KPARTS * 8 + y_hi * 4 + z
    here_grp, across_grp = y_lo * 2 + core, across_lo * 2 + core

    def send_part(k):
        dst = landed.at[mine_slot + k * 8]
        sem = land_sem.at[my_step, k]

        def columns(col):
            return amp.at[:, pl.ds(pl.multiple_of(col * cols + k * part, 128), part)]

        def send(grp, col):
            pltpu.make_async_remote_copy(
                src_ref=columns(col), dst_ref=dst, send_sem=send_sem, recv_sem=sem,
                device_id=(grp, col), device_id_type=MESH,
            ).start()

        @pl.when(own == 1)
        def _():
            pltpu.make_async_copy(columns(c), dst, sem).start()

        @pl.when(own == 0)
        def _():
            send(here_grp, c)

        send(across_grp, x * 8 + across_hi * 4 + z)

        def one(j, _):
            dx = lax.rem(j, 4)
            dz = lax.div(j, 4) + dx
            send(here_grp, lax.rem(x + dx, 4) * 8 + y_hi * 4 + lax.rem(z + dz, 4))
            send(across_grp, lax.rem(x - dx + 4, 4) * 8 + across_hi * 4 + lax.rem(z - dz + 8, 4))
            return 0

        lax.fori_loop(1, 16, one, 0)

    def send_parts(who, first, last):
        if first < last:
            @pl.when(s == who)
            def _():
                lax.fori_loop(first, last, lambda k, _: (send_part(k), 0)[1], 0)

    def block_ref(t, kk, ss, k):
        rows = pl.ds(pl.multiple_of(t * STEP + kk * 2 * BLOCK + ss * BLOCK, 16), BLOCK)
        return panel.at[k // per, rows, pl.ds(pl.multiple_of(k % per * part, 128), part)]

    def forward(t, kk, k, to, sem):
        ref = block_ref(t, kk, s, k)
        return pltpu.make_async_remote_copy(
            src_ref=ref, dst_ref=ref, send_sem=sem, recv_sem=block_sem.at[t, kk * 2 + s, k],
            device_id=to, device_id_type=MESH,
        )

    def wait_block(t, kk, ss, k):
        ref = block_ref(t, kk, ss, k)
        pltpu.make_async_copy(ref, ref, block_sem.at[t, kk * 2 + ss, k]).wait()

    def take(t, k):
        base = (t * KPARTS + k) * 8
        eight = landed.at[pl.ds(base, 8)]
        pltpu.make_async_copy(eight, eight, land_sem.at[t, k]).wait()
        row0 = pl.multiple_of(t * STEP + kind * 2 * BLOCK + s * BLOCK, 16)
        width = min(part, 512)

        def repack(i, _):
            lanes = pl.ds(pl.multiple_of(i * width, width), width)
            to = pl.ds(pl.multiple_of(k % per * part + i * width, width), width)
            for m in range(8):
                wide[pl.ds(m * ROWS, ROWS), :] = landed[base + m, :, lanes].astype(jnp.float32)
            panel[k // per, pl.ds(row0, BLOCK), to] = wide[...].astype(jnp.bfloat16)
            return 0

        lax.fori_loop(0, part // width, repack, 0)
        forward(t, kind, k, pair, pair_send.at[t, k]).start()
        forward(t, kind, k, sibling, sib_send.at[t, 0, k]).start()

    def relay(t, k):
        wait_block(t, 1 - kind, s, k)
        forward(t, 1 - kind, k, sibling, sib_send.at[t, 1, k]).start()

    def wait_sibling(t, k):
        wait_block(t, kind, 1 - s, k)
        wait_block(t, 1 - kind, 1 - s, k)

    def z_copy(t, kk, d):
        return pltpu.make_async_remote_copy(
            src_ref=parts.at[t, kk, lax.rem(z + d, 4)], dst_ref=from_z.at[t, kk, d - 1],
            send_sem=z_send.at[t, kk, d - 1], recv_sem=z_recv.at[t, kk, d - 1],
            device_id=(g, c - z + lax.rem(z + d, 4)), device_id_type=MESH,
        )

    def xb_copy(t, kk, d):
        return pltpu.make_async_remote_copy(
            src_ref=parts_b.at[t, kk, lax.rem(x + d, 4)], dst_ref=from_xb.at[t, kk, d - 1],
            send_sem=xb_send.at[t, kk, d - 1], recv_sem=xb_recv.at[t, kk, d - 1],
            device_id=(g, lax.rem(x + d, 4) * 8 + y_hi * 4 + z), device_id_type=MESH,
        )

    def multiply(t, km, kk=None):
        width = per * part
        last = km == MPARTS - 1
        rows = STEP if kk is None else STEP // 2
        row0 = t * STEP + (0 if kk is None else kk * (2 * BLOCK))
        kinds = (0, 1) if kk is None else (kk,)

        def half(n, _):
            total[0:rows, :] = lax.dot_general(
                panel[km, pl.ds(pl.multiple_of(row0, 16), rows), :],
                integrals[pl.ds(pl.multiple_of(km * width, width), width), pl.ds(pl.multiple_of(n * HALF, HALF), HALF)],
                (((1,), (0,)), ((), ())),
                preferred_element_type=jnp.float32,
            )

            @pl.when(n == 0)
            def _():
                for i, kind_i in enumerate(kinds):
                    for r in range(2):
                        for u in range(2):
                            row = (i * 2 + r) * BLOCK + u * PIECE
                            parts[t, kind_i, 2 * r + u] += total[row:row + PIECE, :]

                @pl.when(last)
                def _():
                    for kind_i in kinds:
                        for d in (2, 1, 3):
                            z_copy(t, kind_i, d).start()

            @pl.when(n == 1)
            def _():
                for i, kind_i in enumerate(kinds):
                    for q in range(4):
                        for r in range(2):
                            for u in range(2):
                                row = (i * 2 + r) * BLOCK + u * PIECE
                                parts_b[t, kind_i, q, 2 * r + u] += total[row:row + PIECE, q * FINE:q * FINE + FINE]

                @pl.when(last)
                def _():
                    for kind_i in kinds:
                        for d in (2, 1, 3):
                            xb_copy(t, kind_i, d).start()

            return 0

        lax.fori_loop(0, 2, half, 0)

    def multiply_steps(first, last, km):
        lax.fori_loop(first, last, lambda t, _: (multiply(t, km), 0)[1], 0)

    u = z % 2

    def owner_x(t, kk):
        return 2 * ((kk + u) % 2) + t // 2

    def x_copy(t, kk):
        d = (owner_x(t, kk) - x + 4) % 4
        place = jnp.maximum(d, 1) - 1
        return d, pltpu.make_async_remote_copy(
            src_ref=reduced.at[t, kk], dst_ref=from_x.at[t % 2, place],
            send_sem=x_send.at[t, kk], recv_sem=x_recv.at[t % 2, place],
            device_id=device(owner_x(t, kk), y, z, s), device_id_type=MESH,
        )

    def y_copy():
        return pltpu.make_async_remote_copy(
            src_ref=summed.at[1], dst_ref=from_y, send_sem=y_send, recv_sem=y_recv,
            device_id=device(x, (y + 2) % 4, z, s), device_id_type=MESH,
        )

    def reduce_z(t, kk):
        for d in range(1, 4):
            z_copy(t, kk, d).wait_recv()
        reduced[t, kk] = 0.5 * (parts[t, kk, z] + from_z[t, kk, 0] + from_z[t, kk, 1] + from_z[t, kk, 2])
        d, cp = x_copy(t, kk)
        pl.when(d != 0)(cp.start)

    def reduce_x(t):
        @pl.when(x % 2 == t // 2)
        def _():
            kk = (x // 2 + u) % 2
            mine = jnp.where(y_hi == t % 2, 0, 1)
            for d in range(3):
                ref = from_x.at[t % 2, d]
                pltpu.make_async_copy(ref, ref, x_recv.at[t % 2, d]).wait()
            summed[mine] = reduced[t, kk] + from_x[t % 2, 0] + from_x[t % 2, 1] + from_x[t % 2, 2]
            pl.when(mine == 1)(y_copy().start)

    def zb_copy(t, kk, d):
        return pltpu.make_async_remote_copy(
            src_ref=reduced_b.at[t, kk, lax.rem(z + d, 4)], dst_ref=from_zb.at[t, kk, d - 1],
            send_sem=zb_send.at[t, kk, d - 1], recv_sem=zb_recv.at[t, kk, d - 1],
            device_id=(g, c - z + lax.rem(z + d, 4)), device_id_type=MESH,
        )

    def reduce_xb(t, kk):
        for d in range(1, 4):
            xb_copy(t, kk, d).wait_recv()
        reduced_b[t, kk] = 0.5 * (
            parts_b[t, kk, x] + from_xb[t, kk, 0] + from_xb[t, kk, 1] + from_xb[t, kk, 2])
        for d in (2, 1, 3):
            zb_copy(t, kk, d).start()

    sender = x * 2 + y_hi

    def xyb_copy(t, kk):
        to_x = owner_x(t, kk)
        here = (to_x == x) & (y_hi == t % 2)
        return here, pltpu.make_async_remote_copy(
            src_ref=summed_b.at[t, kk], dst_ref=from_xyb.at[sender],
            send_sem=xyb_send.at[t, kk], recv_sem=xyb_recv.at[sender],
            device_id=device(to_x, (t % 2) * 2 + y_lo, z, s), device_id_type=MESH,
        )

    def reduce_zb(t, kk):
        for d in range(1, 4):
            zb_copy(t, kk, d).wait_recv()
        summed_b[t, kk] = reduced_b[t, kk, z] + from_zb[t, kk, 0] + from_zb[t, kk, 1] + from_zb[t, kk, 2]
        here, cp = xyb_copy(t, kk)
        pl.when(jnp.logical_not(here))(cp.start)

        @pl.when(here)
        def _():
            from_xyb[sender] = summed_b[t, kk]

    def both_kinds(what, t):
        lax.fori_loop(0, 2, lambda kk, _: (what(t, kk), 0)[1], 0)

    def end_sends(t):
        def one(k, _):
            forward(t, kind, k, pair, pair_send.at[t, k]).wait_send()
            forward(t, kind, k, sibling, sib_send.at[t, 0, k]).wait_send()
            forward(t, 1 - kind, k, sibling, sib_send.at[t, 1, k]).wait_send()
            return 0

        lax.fori_loop(0, KPARTS, one, 0)

    def end_sums_of(t, kk):
        for d in range(1, 4):
            z_copy(t, kk, d).wait_send()
            xb_copy(t, kk, d).wait_send()
            zb_copy(t, kk, d).wait_send()
        d, cp = x_copy(t, kk)
        pl.when(d != 0)(cp.wait_send)
        here, cp = xyb_copy(t, kk)
        pl.when(jnp.logical_not(here))(cp.wait_send)

    def end_sums(t):
        both_kinds(end_sums_of, t)

    def both_first(km):
        for kt in range(km * per, km * per + per):
            wait_sibling(0, kt)
            wait_sibling(1, kt)
        multiply_steps(0, 2, km)

    send_parts(0, 0, AHEAD)
    for k in range(KPARTS):
        take(0, k)
        take(1, k)
        send_parts(0, k + AHEAD, min(k + AHEAD + 1, KPARTS))
        if k >= GATE:
            send_parts(1, k - GATE, k - GATE + 1)
        if k >= LAG:
            relay(0, k - LAG)
            relay(1, k - LAG)
        if k == 0:
            slab_copy(0).start()
            slab_copy(1).start()
        if 1 <= k <= n_slabs // 2:
            turn_slab(2 * k - 2)
            turn_slab(2 * k - 1)
        done = k - LAG - 1
        if done >= 0 and done % per == per - 1:
            both_first(done // per)
    send_parts(1, KPARTS - GATE, KPARTS)
    begun = (KPARTS - LAG - 1) // per
    for k in range(KPARTS):
        take(2, k)
        if k < LAG:
            relay(0, KPARTS - LAG + k)
            relay(1, KPARTS - LAG + k)
        if k >= LAG and (k - LAG) % 2 == 0 and begun + (k - LAG) // 2 < MPARTS:
            both_first(begun + (k - LAG) // 2)

    def third(km, _):
        def one(i, _):
            take(3, km * per + i)
            relay(2, km * per + i)
            return 0

        lax.fori_loop(0, per, one, 0)
        lax.fori_loop(0, per, lambda i, _: (wait_sibling(2, km * per + i), 0)[1], 0)
        multiply(2, km)

        @pl.when(km < 2)
        def _():
            both_kinds(reduce_z, km)
            both_kinds(reduce_xb, km)

        @pl.when(km >= 2)
        def _():
            reduce_x(km - 2)
            both_kinds(reduce_zb, km - 2)

        return 0

    lax.fori_loop(0, MPARTS, third, 0)

    def fourth(km, _):
        @pl.when(km < 2)
        def _():
            def own_kind(i, _):
                m = km * 2 + i
                lax.fori_loop(0, per, lambda i, _: (wait_block(3, kind, 1 - s, m * per + i), 0)[1], 0)
                multiply(3, m, kind)
                return 0

            lax.fori_loop(0, MPARTS // 2, own_kind, 0)

        @pl.when(km == 2)
        def _():
            both_kinds(reduce_z, 2)
            both_kinds(reduce_xb, 2)
            end_sends(0)
            end_sends(1)

        @pl.when(km == 3)
        def _():
            reduce_z(3, kind)
            reduce_xb(3, kind)
            reduce_x(2)
            both_kinds(reduce_zb, 2)
            end_sums(0)
            end_sums(1)

        lax.fori_loop(0, per, lambda i, _: (relay(3, km * per + i), 0)[1], 0)
        lax.fori_loop(0, per, lambda i, _: (wait_block(3, 1 - kind, 1 - s, km * per + i), 0)[1], 0)
        multiply(3, km, 1 - kind)
        return 0

    lax.fori_loop(0, MPARTS, fourth, 0)
    reduce_zb(3, kind)
    reduce_z(3, 1 - kind)
    reduce_xb(3, 1 - kind)
    reduce_x(3)
    reduce_zb(3, 1 - kind)

    y_copy().wait_recv()
    out[:, :HALF] = summed[0] + from_y[...]
    for q in range(4):
        for h in range(2):
            def arrive():
                ref = from_xyb.at[q * 2 + h]
                pltpu.make_async_copy(ref, ref, xyb_recv.at[q * 2 + h]).wait()

            pl.when(sender != q * 2 + h)(arrive)
        out[:, HALF + q * FINE:HALF + q * FINE + FINE] = from_xyb[q * 2] + from_xyb[q * 2 + 1]

    many = 32 * KPARTS

    @pl.when(own == 1)
    def _():
        left = landed.at[pl.ds(0, many - KPARTS)]
        pltpu.make_async_copy(left, left, send_sem).wait()

    @pl.when(own == 0)
    def _():
        left = landed.at[pl.ds(0, many)]
        pltpu.make_async_copy(left, left, send_sem).wait()

    end_sends(2)
    end_sends(3)
    end_sums(2)
    end_sums(3)
    y_copy().wait_send()


def per_device(amplitudes, integrals):
    ab, cols = integrals.shape
    part = cols // KPARTS
    return pl.pallas_call(
        kernel,
        out_shape=jax.ShapeDtypeStruct((PIECE, ab), jnp.float32),
        in_specs=[pl.BlockSpec(memory_space=pl.ANY)] * 2,
        out_specs=pl.BlockSpec(memory_space=pltpu.VMEM),
        scratch_shapes=[
            pltpu.VMEM((2, ab // 8, cols), jnp.bfloat16),
            pltpu.VMEM((cols, ab), jnp.bfloat16),
            pltpu.VMEM((32 * KPARTS, ROWS, part), jnp.bfloat16),
            pltpu.VMEM((BLOCK, min(part, 512)), jnp.float32),
            pltpu.VMEM((MPARTS, STEPS * STEP, cols // MPARTS), jnp.bfloat16),
            pltpu.VMEM((STEP, HALF), jnp.float32),
            pltpu.VMEM((STEPS, 2, 4, PIECE, HALF), jnp.float32),
            pltpu.VMEM((STEPS, 2, 3, PIECE, HALF), jnp.float32),
            pltpu.VMEM((STEPS, 2, PIECE, HALF), jnp.float32),
            pltpu.VMEM((2, 3, PIECE, HALF), jnp.float32),
            pltpu.VMEM((2, PIECE, HALF), jnp.float32),
            pltpu.VMEM((PIECE, HALF), jnp.float32),
            pltpu.VMEM((STEPS, 2, 4, 4, PIECE, FINE), jnp.float32),
            pltpu.VMEM((STEPS, 2, 3, 4, PIECE, FINE), jnp.float32),
            pltpu.VMEM((STEPS, 2, 4, PIECE, FINE), jnp.float32),
            pltpu.VMEM((STEPS, 2, 3, PIECE, FINE), jnp.float32),
            pltpu.VMEM((STEPS, 2, PIECE, FINE), jnp.float32),
            pltpu.VMEM((8, PIECE, FINE), jnp.float32),
            pltpu.SemaphoreType.DMA((2,)),
            pltpu.SemaphoreType.DMA,
            pltpu.SemaphoreType.DMA((STEPS, KPARTS)),
            pltpu.SemaphoreType.DMA((STEPS, KPARTS)),
            pltpu.SemaphoreType.DMA((STEPS, 2, KPARTS)),
            pltpu.SemaphoreType.DMA((STEPS, 4, KPARTS)),
            pltpu.SemaphoreType.DMA((STEPS, 2, 3)),
            pltpu.SemaphoreType.DMA((STEPS, 2, 3)),
            pltpu.SemaphoreType.DMA((STEPS, 2)),
            pltpu.SemaphoreType.DMA((2, 3)),
            pltpu.SemaphoreType.DMA,
            pltpu.SemaphoreType.DMA,
            pltpu.SemaphoreType.DMA((STEPS, 2, 3)),
            pltpu.SemaphoreType.DMA((STEPS, 2, 3)),
            pltpu.SemaphoreType.DMA((STEPS, 2, 3)),
            pltpu.SemaphoreType.DMA((STEPS, 2, 3)),
            pltpu.SemaphoreType.DMA((STEPS, 2)),
            pltpu.SemaphoreType.DMA((8,)),
        ],
        compiler_params=pltpu.CompilerParams(
            collective_id=0, has_side_effects=True, vmem_limit_bytes=60 * 2**20
        ),
        cost_estimate=pl.CostEstimate(
            flops=2 * STEPS * STEP * ab * cols, bytes_accessed=2 * ab * cols, transcendentals=0
        ),
        name="ladder",
    )(amplitudes, integrals)


def solution(mesh):
    return jax.shard_map(
        per_device,
        mesh=mesh,
        in_specs=(P(("grp", "col"), None), P("grp", "col")),
        out_specs=P("col", "grp"),
        check_vma=False,
    )
```

```python
import jax
import jax.numpy as jnp
from jax import lax
from jax.experimental import pallas as pl
from jax.experimental.pallas import tpu as pltpu
from jax.sharding import PartitionSpec as P

MESH = pl.DeviceIdType.MESH
ROWS = 6
BLOCK = 8 * ROWS
STEP = 4 * BLOCK
STEPS = 4
PIECE = 24
KPARTS = 8
MPARTS = 4
HALF = 512
FINE = 128
AHEAD = 5
GATE = 3
LAG = 2


def device(x, y, z, s):
    return ((y % 2) * 2 + s, (x * 2 + y // 2) * 4 + z)


def across(y):
    return (y + 3 + 2 * (y % 2)) % 4


def kernel(amp, integrals_hbm, out, slabs, integrals, landed, wide, panel, total, parts, from_z, reduced, from_x, summed, from_y,
           parts_b, from_xb, reduced_b, from_zb, summed_b, from_xyb,
           load_sem, send_sem, land_sem, pair_send, sib_send, block_sem, z_send, z_recv, x_send, x_recv, y_send, y_recv,
           xb_send, xb_recv, zb_send, zb_recv, xyb_send, xyb_recv):
    g = lax.axis_index("grp")
    c = lax.axis_index("col")
    x, y, z, s = c // 8, (c // 4) % 2 * 2 + g // 2, c % 4, g % 2
    y_hi, y_lo = y // 2, y % 2
    kind = (y_lo + y_hi) % 2
    cols = integrals.shape[0]
    part = cols // KPARTS
    per = KPARTS // MPARTS
    core = x % 2
    own = jnp.where(s == core, 1, 0)
    pair = device(x, y + 1 - 2 * y_lo, z, s)
    sibling = device(x, y, z, 1 - s)

    bar = pltpu.get_barrier_semaphore()

    across_lo, across_hi = 1 - y_lo, 1 - y_hi

    def hello(grp, col):
        pl.semaphore_signal(bar, inc=1, device_id=(grp, col), device_id_type=MESH)

    start_x = x + 1 - own

    def greet(i, _):
        src_x = lax.rem(start_x + 2 * lax.div(i, 4), 4)
        src_z = lax.rem(z + lax.rem(i, 4), 4)
        for src_s in range(2):
            hello(across_lo * 2 + src_s, src_x * 8 + across_hi * 4 + src_z)
            hello(y_lo * 2 + src_s, src_x * 8 + y_hi * 4 + src_z)
        return 0

    lax.fori_loop(1, 8, greet, 0)
    first_x = lax.rem(start_x, 4)
    for src_s in range(2):
        hello(across_lo * 2 + src_s, first_x * 8 + across_hi * 4 + z)
    hello(y_lo * 2 + 1 - s, first_x * 8 + y_hi * 4 + z)

    @pl.when(own == 0)
    def _():
        hello(y_lo * 2 + s, first_x * 8 + y_hi * 4 + z)

    hello(across_lo * 2 + s, c)
    hello(y_lo * 2 + 1 - s, c)
    for d in range(1, 4):
        hello(g, c - z + lax.rem(z + d, 4))
        hello(g, lax.rem(x + d, 4) * 8 + y_hi * 4 + z)
        hello(g, lax.rem(x + d, 4) * 8 + across_hi * 4 + z)
    hello(g, x * 8 + across_hi * 4 + z)
    slab = slabs.shape[1]
    n_slabs = integrals_hbm.shape[0] // slab

    def slab_copy(i):
        rows = pl.ds(pl.multiple_of(i * slab, slab), slab)
        return pltpu.make_async_copy(integrals_hbm.at[rows], slabs.at[i % 2], load_sem.at[i % 2])

    def turn_slab(i):
        slab_copy(i).wait()
        width = 1024

        def one(n, _):
            lanes = pl.ds(pl.multiple_of(n * width, width), width)
            integrals[lanes, pl.ds(i * slab, slab)] = slabs[i % 2, :, lanes].T
            return 0

        lax.fori_loop(0, cols // width, one, 0)
        if i + 2 < n_slabs:
            slab_copy(i + 2).start()

    parts[...] = jnp.zeros_like(parts)
    parts_b[...] = jnp.zeros_like(parts_b)
    pl.semaphore_wait(bar, 44 - own)

    my_step = s * 2 + x // 2

    mine_slot = my_step * KPARTS * 8 + y_hi * 4 + z
    here_grp, across_grp = y_lo * 2 + core, across_lo * 2 + core

    def send_part(k):
        dst = landed.at[mine_slot + k * 8]
        sem = land_sem.at[my_step, k]

        def columns(col):
            return amp.at[:, pl.ds(pl.multiple_of(col * cols + k * part, 128), part)]

        def send(grp, col):
            pltpu.make_async_remote_copy(
                src_ref=columns(col), dst_ref=dst, send_sem=send_sem, recv_sem=sem,
                device_id=(grp, col), device_id_type=MESH,
            ).start()

        @pl.when(own == 1)
        def _():
            pltpu.make_async_copy(columns(c), dst, sem).start()

        @pl.when(own == 0)
        def _():
            send(here_grp, c)

        send(across_grp, x * 8 + across_hi * 4 + z)

        def one(j, _):
            dx = lax.rem(j, 4)
            dz = lax.div(j, 4) + dx
            send(here_grp, lax.rem(x + dx, 4) * 8 + y_hi * 4 + lax.rem(z + dz, 4))
            send(across_grp, lax.rem(x - dx + 4, 4) * 8 + across_hi * 4 + lax.rem(z - dz + 8, 4))
            return 0

        lax.fori_loop(1, 16, one, 0)

    def send_parts(who, first, last):
        if first < last:
            @pl.when(s == who)
            def _():
                lax.fori_loop(first, last, lambda k, _: (send_part(k), 0)[1], 0)

    def block_ref(t, kk, ss, k):
        rows = pl.ds(pl.multiple_of(t * STEP + kk * 2 * BLOCK + ss * BLOCK, 16), BLOCK)
        return panel.at[k // per, rows, pl.ds(pl.multiple_of(k % per * part, 128), part)]

    def forward(t, kk, k, to, sem):
        ref = block_ref(t, kk, s, k)
        return pltpu.make_async_remote_copy(
            src_ref=ref, dst_ref=ref, send_sem=sem, recv_sem=block_sem.at[t, kk * 2 + s, k],
            device_id=to, device_id_type=MESH,
        )

    def wait_block(t, kk, ss, k):
        ref = block_ref(t, kk, ss, k)
        pltpu.make_async_copy(ref, ref, block_sem.at[t, kk * 2 + ss, k]).wait()

    def take(t, k):
        base = (t * KPARTS + k) * 8
        eight = landed.at[pl.ds(base, 8)]
        pltpu.make_async_copy(eight, eight, land_sem.at[t, k]).wait()
        row0 = pl.multiple_of(t * STEP + kind * 2 * BLOCK + s * BLOCK, 16)
        width = min(part, 512)

        def repack(i, _):
            lanes = pl.ds(pl.multiple_of(i * width, width), width)
            to = pl.ds(pl.multiple_of(k % per * part + i * width, width), width)
            for m in range(8):
                wide[pl.ds(m * ROWS, ROWS), :] = landed[base + m, :, lanes].astype(jnp.float32)
            panel[k // per, pl.ds(row0, BLOCK), to] = wide[...].astype(jnp.bfloat16)
            return 0

        lax.fori_loop(0, part // width, repack, 0)
        forward(t, kind, k, pair, pair_send.at[t, k]).start()
        forward(t, kind, k, sibling, sib_send.at[t, 0, k]).start()

    def relay(t, k):
        wait_block(t, 1 - kind, s, k)
        forward(t, 1 - kind, k, sibling, sib_send.at[t, 1, k]).start()

    def wait_sibling(t, k):
        wait_block(t, kind, 1 - s, k)
        wait_block(t, 1 - kind, 1 - s, k)

    def z_copy(t, kk, d):
        return pltpu.make_async_remote_copy(
            src_ref=parts.at[t, kk, lax.rem(z + d, 4)], dst_ref=from_z.at[t, kk, d - 1],
            send_sem=z_send.at[t, kk, d - 1], recv_sem=z_recv.at[t, kk, d - 1],
            device_id=(g, c - z + lax.rem(z + d, 4)), device_id_type=MESH,
        )

    def xb_copy(t, kk, d):
        return pltpu.make_async_remote_copy(
            src_ref=parts_b.at[t, kk, lax.rem(x + d, 4)], dst_ref=from_xb.at[t, kk, d - 1],
            send_sem=xb_send.at[t, kk, d - 1], recv_sem=xb_recv.at[t, kk, d - 1],
            device_id=(g, lax.rem(x + d, 4) * 8 + y_hi * 4 + z), device_id_type=MESH,
        )

    def multiply(t, km, kk=None):
        width = per * part
        last = km == MPARTS - 1
        rows = STEP if kk is None else STEP // 2
        row0 = t * STEP + (0 if kk is None else kk * (2 * BLOCK))
        kinds = (0, 1) if kk is None else (kk,)

        def half(n, _):
            total[0:rows, :] = lax.dot_general(
                panel[km, pl.ds(pl.multiple_of(row0, 16), rows), :],
                integrals[pl.ds(pl.multiple_of(km * width, width), width), pl.ds(pl.multiple_of(n * HALF, HALF), HALF)],
                (((1,), (0,)), ((), ())),
                preferred_element_type=jnp.float32,
            )

            @pl.when(n == 0)
            def _():
                for i, kind_i in enumerate(kinds):
                    for r in range(2):
                        for u in range(2):
                            row = (i * 2 + r) * BLOCK + u * PIECE
                            parts[t, kind_i, 2 * r + u] += total[row:row + PIECE, :]

                @pl.when(last)
                def _():
                    for kind_i in kinds:
                        for d in (2, 1, 3):
                            z_copy(t, kind_i, d).start()

            @pl.when(n == 1)
            def _():
                for i, kind_i in enumerate(kinds):
                    for q in range(4):
                        for r in range(2):
                            for u in range(2):
                                row = (i * 2 + r) * BLOCK + u * PIECE
                                parts_b[t, kind_i, q, 2 * r + u] += total[row:row + PIECE, q * FINE:q * FINE + FINE]

                @pl.when(last)
                def _():
                    for kind_i in kinds:
                        for d in (2, 1, 3):
                            xb_copy(t, kind_i, d).start()

            return 0

        lax.fori_loop(0, 2, half, 0)

    def multiply_steps(first, last, km):
        lax.fori_loop(first, last, lambda t, _: (multiply(t, km), 0)[1], 0)

    u = z % 2

    def owner_x(t, kk):
        return 2 * ((kk + u) % 2) + t // 2

    def x_copy(t, kk):
        d = (owner_x(t, kk) - x + 4) % 4
        place = jnp.maximum(d, 1) - 1
        return d, pltpu.make_async_remote_copy(
            src_ref=reduced.at[t, kk], dst_ref=from_x.at[t % 2, place],
            send_sem=x_send.at[t, kk], recv_sem=x_recv.at[t % 2, place],
            device_id=device(owner_x(t, kk), y, z, s), device_id_type=MESH,
        )

    def y_copy():
        return pltpu.make_async_remote_copy(
            src_ref=summed.at[1], dst_ref=from_y, send_sem=y_send, recv_sem=y_recv,
            device_id=device(x, (y + 2) % 4, z, s), device_id_type=MESH,
        )

    def reduce_z(t, kk):
        for d in range(1, 4):
            z_copy(t, kk, d).wait_recv()
        reduced[t, kk] = 0.5 * (parts[t, kk, z] + from_z[t, kk, 0] + from_z[t, kk, 1] + from_z[t, kk, 2])
        d, cp = x_copy(t, kk)
        pl.when(d != 0)(cp.start)

    def reduce_x(t):
        @pl.when(x % 2 == t // 2)
        def _():
            kk = (x // 2 + u) % 2
            mine = jnp.where(y_hi == t % 2, 0, 1)
            for d in range(3):
                ref = from_x.at[t % 2, d]
                pltpu.make_async_copy(ref, ref, x_recv.at[t % 2, d]).wait()
            summed[mine] = reduced[t, kk] + from_x[t % 2, 0] + from_x[t % 2, 1] + from_x[t % 2, 2]
            pl.when(mine == 1)(y_copy().start)

    def zb_copy(t, kk, d):
        return pltpu.make_async_remote_copy(
            src_ref=reduced_b.at[t, kk, lax.rem(z + d, 4)], dst_ref=from_zb.at[t, kk, d - 1],
            send_sem=zb_send.at[t, kk, d - 1], recv_sem=zb_recv.at[t, kk, d - 1],
            device_id=(g, c - z + lax.rem(z + d, 4)), device_id_type=MESH,
        )

    def reduce_xb(t, kk):
        for d in range(1, 4):
            xb_copy(t, kk, d).wait_recv()
        reduced_b[t, kk] = 0.5 * (
            parts_b[t, kk, x] + from_xb[t, kk, 0] + from_xb[t, kk, 1] + from_xb[t, kk, 2])
        for d in (2, 1, 3):
            zb_copy(t, kk, d).start()

    sender = x * 2 + y_hi

    def xyb_copy(t, kk):
        to_x = owner_x(t, kk)
        here = (to_x == x) & (y_hi == t % 2)
        return here, pltpu.make_async_remote_copy(
            src_ref=summed_b.at[t, kk], dst_ref=from_xyb.at[sender],
            send_sem=xyb_send.at[t, kk], recv_sem=xyb_recv.at[sender],
            device_id=device(to_x, (t % 2) * 2 + y_lo, z, s), device_id_type=MESH,
        )

    def reduce_zb(t, kk):
        for d in range(1, 4):
            zb_copy(t, kk, d).wait_recv()
        summed_b[t, kk] = reduced_b[t, kk, z] + from_zb[t, kk, 0] + from_zb[t, kk, 1] + from_zb[t, kk, 2]
        here, cp = xyb_copy(t, kk)
        pl.when(jnp.logical_not(here))(cp.start)

        @pl.when(here)
        def _():
            from_xyb[sender] = summed_b[t, kk]

    def both_kinds(what, t):
        lax.fori_loop(0, 2, lambda kk, _: (what(t, kk), 0)[1], 0)

    def end_sends(t):
        def one(k, _):
            forward(t, kind, k, pair, pair_send.at[t, k]).wait_send()
            forward(t, kind, k, sibling, sib_send.at[t, 0, k]).wait_send()
            forward(t, 1 - kind, k, sibling, sib_send.at[t, 1, k]).wait_send()
            return 0

        lax.fori_loop(0, KPARTS, one, 0)

    def end_sums_of(t, kk):
        for d in range(1, 4):
            z_copy(t, kk, d).wait_send()
            xb_copy(t, kk, d).wait_send()
            zb_copy(t, kk, d).wait_send()
        d, cp = x_copy(t, kk)
        pl.when(d != 0)(cp.wait_send)
        here, cp = xyb_copy(t, kk)
        pl.when(jnp.logical_not(here))(cp.wait_send)

    def end_sums(t):
        both_kinds(end_sums_of, t)

    def end_direct():
        many = 32 * KPARTS

        @pl.when(own == 1)
        def _():
            left = landed.at[pl.ds(0, many - KPARTS)]
            pltpu.make_async_copy(left, left, send_sem).wait()

        @pl.when(own == 0)
        def _():
            left = landed.at[pl.ds(0, many)]
            pltpu.make_async_copy(left, left, send_sem).wait()

    def both_first(km):
        for kt in range(km * per, km * per + per):
            wait_sibling(0, kt)
            wait_sibling(1, kt)
        multiply_steps(0, 2, km)

    send_parts(0, 0, AHEAD)
    for k in range(KPARTS):
        take(0, k)
        take(1, k)
        send_parts(0, k + AHEAD, min(k + AHEAD + 1, KPARTS))
        if k >= GATE:
            send_parts(1, k - GATE, k - GATE + 1)
        if k >= LAG:
            relay(0, k - LAG)
            relay(1, k - LAG)
        if k == 0:
            slab_copy(0).start()
            slab_copy(1).start()
        if 1 <= k <= n_slabs // 2:
            turn_slab(2 * k - 2)
            turn_slab(2 * k - 1)
        done = k - LAG - 1
        if done >= 0 and done % per == per - 1:
            both_first(done // per)
    send_parts(1, KPARTS - GATE, KPARTS)
    begun = (KPARTS - LAG - 1) // per
    for k in range(KPARTS):
        take(2, k)
        if k < LAG:
            relay(0, KPARTS - LAG + k)
            relay(1, KPARTS - LAG + k)
        if k >= LAG and (k - LAG) % 2 == 0 and begun + (k - LAG) // 2 < MPARTS:
            both_first(begun + (k - LAG) // 2)

    def third(km, _):
        def one(i, _):
            take(3, km * per + i)
            relay(2, km * per + i)
            return 0

        lax.fori_loop(0, per, one, 0)
        lax.fori_loop(0, per, lambda i, _: (wait_sibling(2, km * per + i), 0)[1], 0)
        multiply(2, km)

        @pl.when(km < 2)
        def _():
            both_kinds(reduce_z, km)
            both_kinds(reduce_xb, km)

        @pl.when(km >= 2)
        def _():
            reduce_x(km - 2)
            both_kinds(reduce_zb, km - 2)

        return 0

    lax.fori_loop(0, MPARTS, third, 0)

    def fourth(km, _):
        def relays(first, last):
            lax.fori_loop(first, last, lambda i, _: (relay(3, km * per + i), 0)[1], 0)

        relays(0, 1)

        @pl.when(km < 2)
        def _():
            def own_kind(i, _):
                m = km * 2 + i
                lax.fori_loop(0, per, lambda i, _: (wait_block(3, kind, 1 - s, m * per + i), 0)[1], 0)
                multiply(3, m, kind)
                return 0

            lax.fori_loop(0, MPARTS // 2, own_kind, 0)

        @pl.when(km == 2)
        def _():
            both_kinds(reduce_z, 2)
            both_kinds(reduce_xb, 2)
            end_sends(0)
            end_sends(1)

        @pl.when(km == 3)
        def _():
            reduce_z(3, kind)
            reduce_xb(3, kind)
            reduce_x(2)
            both_kinds(reduce_zb, 2)

        relays(1, per)
        lax.fori_loop(0, per, lambda i, _: (wait_block(3, 1 - kind, 1 - s, km * per + i), 0)[1], 0)
        multiply(3, km, 1 - kind)
        return 0

    lax.fori_loop(0, MPARTS, fourth, 0)
    reduce_zb(3, kind)
    end_sums(0)
    end_sends(2)
    reduce_z(3, 1 - kind)
    reduce_xb(3, 1 - kind)
    end_sums(1)
    reduce_x(3)
    reduce_zb(3, 1 - kind)
    end_sends(3)
    end_sums(2)
    end_direct()

    y_copy().wait_recv()
    out[:, :HALF] = summed[0] + from_y[...]
    for q in range(4):
        for h in range(2):
            def arrive():
                ref = from_xyb.at[q * 2 + h]
                pltpu.make_async_copy(ref, ref, xyb_recv.at[q * 2 + h]).wait()

            pl.when(sender != q * 2 + h)(arrive)
        out[:, HALF + q * FINE:HALF + q * FINE + FINE] = from_xyb[q * 2] + from_xyb[q * 2 + 1]

    both_kinds(end_sums_of, 3)
    y_copy().wait_send()


def per_device(amplitudes, integrals):
    ab, cols = integrals.shape
    part = cols // KPARTS
    return pl.pallas_call(
        kernel,
        out_shape=jax.ShapeDtypeStruct((PIECE, ab), jnp.float32),
        in_specs=[pl.BlockSpec(memory_space=pl.ANY)] * 2,
        out_specs=pl.BlockSpec(memory_space=pltpu.VMEM),
        scratch_shapes=[
            pltpu.VMEM((2, ab // 8, cols), jnp.bfloat16),
            pltpu.VMEM((cols, ab), jnp.bfloat16),
            pltpu.VMEM((32 * KPARTS, ROWS, part), jnp.bfloat16),
            pltpu.VMEM((BLOCK, min(part, 512)), jnp.float32),
            pltpu.VMEM((MPARTS, STEPS * STEP, cols // MPARTS), jnp.bfloat16),
            pltpu.VMEM((STEP, HALF), jnp.float32),
            pltpu.VMEM((STEPS, 2, 4, PIECE, HALF), jnp.float32),
            pltpu.VMEM((STEPS, 2, 3, PIECE, HALF), jnp.float32),
            pltpu.VMEM((STEPS, 2, PIECE, HALF), jnp.float32),
            pltpu.VMEM((2, 3, PIECE, HALF), jnp.float32),
            pltpu.VMEM((2, PIECE, HALF), jnp.float32),
            pltpu.VMEM((PIECE, HALF), jnp.float32),
            pltpu.VMEM((STEPS, 2, 4, 4, PIECE, FINE), jnp.float32),
            pltpu.VMEM((STEPS, 2, 3, 4, PIECE, FINE), jnp.float32),
            pltpu.VMEM((STEPS, 2, 4, PIECE, FINE), jnp.float32),
            pltpu.VMEM((STEPS, 2, 3, PIECE, FINE), jnp.float32),
            pltpu.VMEM((STEPS, 2, PIECE, FINE), jnp.float32),
            pltpu.VMEM((8, PIECE, FINE), jnp.float32),
            pltpu.SemaphoreType.DMA((2,)),
            pltpu.SemaphoreType.DMA,
            pltpu.SemaphoreType.DMA((STEPS, KPARTS)),
            pltpu.SemaphoreType.DMA((STEPS, KPARTS)),
            pltpu.SemaphoreType.DMA((STEPS, 2, KPARTS)),
            pltpu.SemaphoreType.DMA((STEPS, 4, KPARTS)),
            pltpu.SemaphoreType.DMA((STEPS, 2, 3)),
            pltpu.SemaphoreType.DMA((STEPS, 2, 3)),
            pltpu.SemaphoreType.DMA((STEPS, 2)),
            pltpu.SemaphoreType.DMA((2, 3)),
            pltpu.SemaphoreType.DMA,
            pltpu.SemaphoreType.DMA,
            pltpu.SemaphoreType.DMA((STEPS, 2, 3)),
            pltpu.SemaphoreType.DMA((STEPS, 2, 3)),
            pltpu.SemaphoreType.DMA((STEPS, 2, 3)),
            pltpu.SemaphoreType.DMA((STEPS, 2, 3)),
            pltpu.SemaphoreType.DMA((STEPS, 2)),
            pltpu.SemaphoreType.DMA((8,)),
        ],
        compiler_params=pltpu.CompilerParams(
            collective_id=0, has_side_effects=True, vmem_limit_bytes=60 * 2**20
        ),
        cost_estimate=pl.CostEstimate(
            flops=2 * STEPS * STEP * ab * cols, bytes_accessed=2 * ab * cols, transcendentals=0
        ),
        name="ladder",
    )(amplitudes, integrals)


def solution(mesh):
    return jax.shard_map(
        per_device,
        mesh=mesh,
        in_specs=(P(("grp", "col"), None), P("grp", "col")),
        out_specs=P("col", "grp"),
        check_vma=False,
    )
```

```python
import jax
import jax.numpy as jnp
from jax import lax
from jax.experimental import pallas as pl
from jax.experimental.pallas import tpu as pltpu
from jax.sharding import PartitionSpec as P

MESH = pl.DeviceIdType.MESH
ROWS = 6
BLOCK = 8 * ROWS
STEP = 4 * BLOCK
STEPS = 4
PIECE = 24
KPARTS = 8
MPARTS = 4
HALF = 512
FINE = 128
AHEAD = 5
GATE = 3
LAG = 2


def device(x, y, z, s):
    return ((y % 2) * 2 + s, (x * 2 + y // 2) * 4 + z)


def across(y):
    return (y + 3 + 2 * (y % 2)) % 4


def kernel(amp, integrals_hbm, out, slabs, integrals, landed, wide, panel, total, parts, from_z, reduced, from_x, summed, from_y,
           parts_b, from_xb, reduced_b, from_zb, summed_b, from_xyb,
           load_sem, send_sem, land_sem, pair_send, sib_send, block_sem, z_send, z_recv, x_send, x_recv, y_send, y_recv,
           xb_send, xb_recv, zb_send, zb_recv, xyb_send, xyb_recv):
    g = lax.axis_index("grp")
    c = lax.axis_index("col")
    x, y, z, s = c // 8, (c // 4) % 2 * 2 + g // 2, c % 4, g % 2
    y_hi, y_lo = y // 2, y % 2
    kind = (y_lo + y_hi) % 2
    cols = integrals.shape[0]
    part = cols // KPARTS
    per = KPARTS // MPARTS
    core = x % 2
    own = jnp.where(s == core, 1, 0)
    pair = device(x, y + 1 - 2 * y_lo, z, s)
    sibling = device(x, y, z, 1 - s)

    bar = pltpu.get_barrier_semaphore()

    across_lo, across_hi = 1 - y_lo, 1 - y_hi

    def hello(grp, col):
        pl.semaphore_signal(bar, inc=1, device_id=(grp, col), device_id_type=MESH)

    start_x = x + 1 - own

    def greet(i, _):
        src_x = lax.rem(start_x + 2 * lax.div(i, 4), 4)
        src_z = lax.rem(z + lax.rem(i, 4), 4)
        for src_s in range(2):
            hello(across_lo * 2 + src_s, src_x * 8 + across_hi * 4 + src_z)
            hello(y_lo * 2 + src_s, src_x * 8 + y_hi * 4 + src_z)
        return 0

    lax.fori_loop(1, 8, greet, 0)
    first_x = lax.rem(start_x, 4)
    for src_s in range(2):
        hello(across_lo * 2 + src_s, first_x * 8 + across_hi * 4 + z)
    hello(y_lo * 2 + 1 - s, first_x * 8 + y_hi * 4 + z)

    @pl.when(own == 0)
    def _():
        hello(y_lo * 2 + s, first_x * 8 + y_hi * 4 + z)

    hello(across_lo * 2 + s, c)
    hello(y_lo * 2 + 1 - s, c)
    for d in range(1, 4):
        hello(g, c - z + lax.rem(z + d, 4))
        hello(g, lax.rem(x + d, 4) * 8 + y_hi * 4 + z)
        hello(g, lax.rem(x + d, 4) * 8 + across_hi * 4 + z)
    hello(g, x * 8 + across_hi * 4 + z)
    slab = slabs.shape[1]
    n_slabs = integrals_hbm.shape[0] // slab

    def slab_copy(i):
        rows = pl.ds(pl.multiple_of(i * slab, slab), slab)
        return pltpu.make_async_copy(integrals_hbm.at[rows], slabs.at[i % 2], load_sem.at[i % 2])

    def turn_slab(i):
        slab_copy(i).wait()
        width = 1024

        def one(n, _):
            lanes = pl.ds(pl.multiple_of(n * width, width), width)
            integrals[lanes, pl.ds(i * slab, slab)] = slabs[i % 2, :, lanes].T
            return 0

        lax.fori_loop(0, cols // width, one, 0)
        if i + 2 < n_slabs:
            slab_copy(i + 2).start()

    parts[...] = jnp.zeros_like(parts)
    parts_b[...] = jnp.zeros_like(parts_b)
    pl.semaphore_wait(bar, 44 - own)

    my_step = s * 2 + x // 2

    mine_slot = my_step * KPARTS * 8 + y_hi * 4 + z
    here_grp, across_grp = y_lo * 2 + core, across_lo * 2 + core

    def send_part(k):
        dst = landed.at[mine_slot + k * 8]
        sem = land_sem.at[my_step, k]

        def columns(col):
            return amp.at[:, pl.ds(pl.multiple_of(col * cols + k * part, 128), part)]

        def send(grp, col):
            pltpu.make_async_remote_copy(
                src_ref=columns(col), dst_ref=dst, send_sem=send_sem, recv_sem=sem,
                device_id=(grp, col), device_id_type=MESH,
            ).start()

        @pl.when(own == 1)
        def _():
            pltpu.make_async_copy(columns(c), dst, sem).start()

        @pl.when(own == 0)
        def _():
            send(here_grp, c)

        send(across_grp, x * 8 + across_hi * 4 + z)

        def one(j, _):
            dx = lax.rem(j, 4)
            dz = lax.div(j, 4) + dx
            send(here_grp, lax.rem(x + dx, 4) * 8 + y_hi * 4 + lax.rem(z + dz, 4))
            send(across_grp, lax.rem(x - dx + 4, 4) * 8 + across_hi * 4 + lax.rem(z - dz + 8, 4))
            return 0

        lax.fori_loop(1, 16, one, 0)

    def send_parts(who, first, last):
        if first < last:
            @pl.when(s == who)
            def _():
                lax.fori_loop(first, last, lambda k, _: (send_part(k), 0)[1], 0)

    def block_ref(t, kk, ss, k):
        rows = pl.ds(pl.multiple_of(t * STEP + kk * 2 * BLOCK + ss * BLOCK, 16), BLOCK)
        return panel.at[k // per, rows, pl.ds(pl.multiple_of(k % per * part, 128), part)]

    def forward(t, kk, k, to, sem):
        ref = block_ref(t, kk, s, k)
        return pltpu.make_async_remote_copy(
            src_ref=ref, dst_ref=ref, send_sem=sem, recv_sem=block_sem.at[t, kk * 2 + s, k],
            device_id=to, device_id_type=MESH,
        )

    def wait_block(t, kk, ss, k):
        ref = block_ref(t, kk, ss, k)
        pltpu.make_async_copy(ref, ref, block_sem.at[t, kk * 2 + ss, k]).wait()

    def take(t, k):
        base = (t * KPARTS + k) * 8
        eight = landed.at[pl.ds(base, 8)]
        pltpu.make_async_copy(eight, eight, land_sem.at[t, k]).wait()
        row0 = pl.multiple_of(t * STEP + kind * 2 * BLOCK + s * BLOCK, 16)
        width = min(part, 512)

        def repack(i, _):
            lanes = pl.ds(pl.multiple_of(i * width, width), width)
            to = pl.ds(pl.multiple_of(k % per * part + i * width, width), width)
            for m in range(8):
                wide[pl.ds(m * ROWS, ROWS), :] = landed[base + m, :, lanes].astype(jnp.float32)
            panel[k // per, pl.ds(row0, BLOCK), to] = wide[...].astype(jnp.bfloat16)
            return 0

        lax.fori_loop(0, part // width, repack, 0)
        forward(t, kind, k, pair, pair_send.at[t, k]).start()
        forward(t, kind, k, sibling, sib_send.at[t, 0, k]).start()

    def relay(t, k):
        wait_block(t, 1 - kind, s, k)
        forward(t, 1 - kind, k, sibling, sib_send.at[t, 1, k]).start()

    def wait_sibling(t, k):
        wait_block(t, kind, 1 - s, k)
        wait_block(t, 1 - kind, 1 - s, k)

    def z_copy(t, kk, d):
        return pltpu.make_async_remote_copy(
            src_ref=parts.at[t, kk, lax.rem(z + d, 4)], dst_ref=from_z.at[t, kk, d - 1],
            send_sem=z_send.at[t, kk, d - 1], recv_sem=z_recv.at[t, kk, d - 1],
            device_id=(g, c - z + lax.rem(z + d, 4)), device_id_type=MESH,
        )

    def xb_copy(t, kk, d):
        return pltpu.make_async_remote_copy(
            src_ref=parts_b.at[t, kk, lax.rem(x + d, 4)], dst_ref=from_xb.at[t, kk, d - 1],
            send_sem=xb_send.at[t, kk, d - 1], recv_sem=xb_recv.at[t, kk, d - 1],
            device_id=(g, lax.rem(x + d, 4) * 8 + y_hi * 4 + z), device_id_type=MESH,
        )

    def multiply(t, km, kk=None):
        width = per * part
        last = km == MPARTS - 1
        rows = STEP if kk is None else STEP // 2
        row0 = t * STEP + (0 if kk is None else kk * (2 * BLOCK))
        kinds = (0, 1) if kk is None else (kk,)

        def half(n, _):
            total[0:rows, :] = lax.dot_general(
                panel[km, pl.ds(pl.multiple_of(row0, 16), rows), :],
                integrals[pl.ds(pl.multiple_of(km * width, width), width), pl.ds(pl.multiple_of(n * HALF, HALF), HALF)],
                (((1,), (0,)), ((), ())),
                preferred_element_type=jnp.float32,
            )

            @pl.when(n == 0)
            def _():
                for i, kind_i in enumerate(kinds):
                    for r in range(2):
                        for u in range(2):
                            row = (i * 2 + r) * BLOCK + u * PIECE
                            parts[t, kind_i, 2 * r + u] += total[row:row + PIECE, :]

                @pl.when(last)
                def _():
                    for kind_i in kinds:
                        for d in (2, 1, 3):
                            z_copy(t, kind_i, d).start()

            @pl.when(n == 1)
            def _():
                for i, kind_i in enumerate(kinds):
                    for q in range(4):
                        for r in range(2):
                            for u in range(2):
                                row = (i * 2 + r) * BLOCK + u * PIECE
                                parts_b[t, kind_i, q, 2 * r + u] += total[row:row + PIECE, q * FINE:q * FINE + FINE]

                @pl.when(last)
                def _():
                    for kind_i in kinds:
                        for d in (2, 1, 3):
                            xb_copy(t, kind_i, d).start()

            return 0

        lax.fori_loop(0, 2, half, 0)

    def multiply_steps(first, last, km):
        lax.fori_loop(first, last, lambda t, _: (multiply(t, km), 0)[1], 0)

    u = z % 2

    def owner_x(t, kk):
        return 2 * ((kk + u) % 2) + t // 2

    def x_copy(t, kk):
        d = (owner_x(t, kk) - x + 4) % 4
        place = jnp.maximum(d, 1) - 1
        return d, pltpu.make_async_remote_copy(
            src_ref=reduced.at[t, kk], dst_ref=from_x.at[t % 2, place],
            send_sem=x_send.at[t, kk], recv_sem=x_recv.at[t % 2, place],
            device_id=device(owner_x(t, kk), y, z, s), device_id_type=MESH,
        )

    def y_copy():
        return pltpu.make_async_remote_copy(
            src_ref=summed.at[1], dst_ref=from_y, send_sem=y_send, recv_sem=y_recv,
            device_id=device(x, (y + 2) % 4, z, s), device_id_type=MESH,
        )

    def reduce_z(t, kk):
        for d in range(1, 4):
            z_copy(t, kk, d).wait_recv()
        reduced[t, kk] = 0.5 * (parts[t, kk, z] + from_z[t, kk, 0] + from_z[t, kk, 1] + from_z[t, kk, 2])
        d, cp = x_copy(t, kk)
        pl.when(d != 0)(cp.start)

    def reduce_x(t):
        @pl.when(x % 2 == t // 2)
        def _():
            kk = (x // 2 + u) % 2
            mine = jnp.where(y_hi == t % 2, 0, 1)
            for d in range(3):
                ref = from_x.at[t % 2, d]
                pltpu.make_async_copy(ref, ref, x_recv.at[t % 2, d]).wait()
            summed[mine] = reduced[t, kk] + from_x[t % 2, 0] + from_x[t % 2, 1] + from_x[t % 2, 2]
            pl.when(mine == 1)(y_copy().start)

    def zb_copy(t, kk, d):
        return pltpu.make_async_remote_copy(
            src_ref=reduced_b.at[t, kk, lax.rem(z + d, 4)], dst_ref=from_zb.at[t, kk, d - 1],
            send_sem=zb_send.at[t, kk, d - 1], recv_sem=zb_recv.at[t, kk, d - 1],
            device_id=(g, c - z + lax.rem(z + d, 4)), device_id_type=MESH,
        )

    def reduce_xb(t, kk):
        for d in range(1, 4):
            xb_copy(t, kk, d).wait_recv()
        reduced_b[t, kk] = 0.5 * (
            parts_b[t, kk, x] + from_xb[t, kk, 0] + from_xb[t, kk, 1] + from_xb[t, kk, 2])
        for d in (2, 1, 3):
            zb_copy(t, kk, d).start()

    sender = x * 2 + y_hi

    def xyb_copy(t, kk):
        to_x = owner_x(t, kk)
        here = (to_x == x) & (y_hi == t % 2)
        return here, pltpu.make_async_remote_copy(
            src_ref=summed_b.at[t, kk], dst_ref=from_xyb.at[sender],
            send_sem=xyb_send.at[t, kk], recv_sem=xyb_recv.at[sender],
            device_id=device(to_x, (t % 2) * 2 + y_lo, z, s), device_id_type=MESH,
        )

    def reduce_zb(t, kk):
        for d in range(1, 4):
            zb_copy(t, kk, d).wait_recv()
        summed_b[t, kk] = reduced_b[t, kk, z] + from_zb[t, kk, 0] + from_zb[t, kk, 1] + from_zb[t, kk, 2]
        here, cp = xyb_copy(t, kk)
        pl.when(jnp.logical_not(here))(cp.start)

        @pl.when(here)
        def _():
            from_xyb[sender] = summed_b[t, kk]

    def both_kinds(what, t):
        lax.fori_loop(0, 2, lambda kk, _: (what(t, kk), 0)[1], 0)

    def end_sends(t):
        def one(k, _):
            forward(t, kind, k, pair, pair_send.at[t, k]).wait_send()
            forward(t, kind, k, sibling, sib_send.at[t, 0, k]).wait_send()
            forward(t, 1 - kind, k, sibling, sib_send.at[t, 1, k]).wait_send()
            return 0

        lax.fori_loop(0, KPARTS, one, 0)

    def end_sums_of(t, kk):
        for d in range(1, 4):
            z_copy(t, kk, d).wait_send()
            xb_copy(t, kk, d).wait_send()
            zb_copy(t, kk, d).wait_send()
        d, cp = x_copy(t, kk)
        pl.when(d != 0)(cp.wait_send)
        here, cp = xyb_copy(t, kk)
        pl.when(jnp.logical_not(here))(cp.wait_send)

    def end_sums(t):
        both_kinds(end_sums_of, t)

    def end_direct():
        many = 32 * KPARTS

        @pl.when(own == 1)
        def _():
            left = landed.at[pl.ds(0, many - KPARTS)]
            pltpu.make_async_copy(left, left, send_sem).wait()

        @pl.when(own == 0)
        def _():
            left = landed.at[pl.ds(0, many)]
            pltpu.make_async_copy(left, left, send_sem).wait()

    def both_first(km):
        for kt in range(km * per, km * per + per):
            wait_sibling(0, kt)
            wait_sibling(1, kt)
        multiply_steps(0, 2, km)

    send_parts(0, 0, AHEAD)
    for k in range(KPARTS):
        take(0, k)
        take(1, k)
        send_parts(0, k + AHEAD, min(k + AHEAD + 1, KPARTS))
        if k >= GATE:
            send_parts(1, k - GATE, k - GATE + 1)
        if k >= LAG:
            relay(0, k - LAG)
            relay(1, k - LAG)
        if k == 0:
            slab_copy(0).start()
            slab_copy(1).start()
        if 1 <= k <= n_slabs // 2:
            turn_slab(2 * k - 2)
            turn_slab(2 * k - 1)
        done = k - LAG - 1
        if done >= 0 and done % per == per - 1:
            both_first(done // per)
    send_parts(1, KPARTS - GATE, KPARTS)
    begun = (KPARTS - LAG - 1) // per
    for k in range(KPARTS):
        take(2, k)
        if k < LAG:
            relay(0, KPARTS - LAG + k)
            relay(1, KPARTS - LAG + k)
        if k >= LAG and (k - LAG) % 2 == 0 and begun + (k - LAG) // 2 < MPARTS:
            both_first(begun + (k - LAG) // 2)

    def third(km, _):
        @pl.when(km < MPARTS // 2)
        def _():
            lax.fori_loop(0, 2 * per, lambda i, _: (take(3, km * 2 * per + i), 0)[1], 0)

        lax.fori_loop(0, per, lambda i, _: (relay(2, km * per + i), 0)[1], 0)
        lax.fori_loop(0, per, lambda i, _: (wait_sibling(2, km * per + i), 0)[1], 0)
        multiply(2, km)

        @pl.when(km < 2)
        def _():
            both_kinds(reduce_z, km)
            both_kinds(reduce_xb, km)

        @pl.when(km >= 2)
        def _():
            reduce_x(km - 2)
            both_kinds(reduce_zb, km - 2)

        return 0

    lax.fori_loop(0, MPARTS, third, 0)

    def fourth(km, _):
        def relays(first, last):
            lax.fori_loop(first, last, lambda i, _: (relay(3, km * per + i), 0)[1], 0)

        relays(0, 1)

        @pl.when(km < 2)
        def _():
            def own_kind(i, _):
                m = km * 2 + i
                lax.fori_loop(0, per, lambda i, _: (wait_block(3, kind, 1 - s, m * per + i), 0)[1], 0)
                multiply(3, m, kind)
                return 0

            lax.fori_loop(0, MPARTS // 2, own_kind, 0)

        @pl.when(km == 2)
        def _():
            both_kinds(reduce_z, 2)
            both_kinds(reduce_xb, 2)
            end_sends(0)
            end_sends(1)

        @pl.when(km == 3)
        def _():
            reduce_z(3, kind)
            reduce_xb(3, kind)
            reduce_x(2)
            both_kinds(reduce_zb, 2)

        relays(1, per)
        lax.fori_loop(0, per, lambda i, _: (wait_block(3, 1 - kind, 1 - s, km * per + i), 0)[1], 0)
        multiply(3, km, 1 - kind)
        return 0

    lax.fori_loop(0, MPARTS, fourth, 0)
    reduce_zb(3, kind)
    end_sums(0)
    end_sends(2)
    reduce_z(3, 1 - kind)
    reduce_xb(3, 1 - kind)
    end_sums(1)
    reduce_x(3)
    reduce_zb(3, 1 - kind)
    end_sends(3)
    end_sums(2)
    end_direct()

    y_copy().wait_recv()
    out[:, :HALF] = summed[0] + from_y[...]
    for q in range(4):
        for h in range(2):
            def arrive():
                ref = from_xyb.at[q * 2 + h]
                pltpu.make_async_copy(ref, ref, xyb_recv.at[q * 2 + h]).wait()

            pl.when(sender != q * 2 + h)(arrive)
        out[:, HALF + q * FINE:HALF + q * FINE + FINE] = from_xyb[q * 2] + from_xyb[q * 2 + 1]

    both_kinds(end_sums_of, 3)
    y_copy().wait_send()


def per_device(amplitudes, integrals):
    ab, cols = integrals.shape
    part = cols // KPARTS
    return pl.pallas_call(
        kernel,
        out_shape=jax.ShapeDtypeStruct((PIECE, ab), jnp.float32),
        in_specs=[pl.BlockSpec(memory_space=pl.ANY)] * 2,
        out_specs=pl.BlockSpec(memory_space=pltpu.VMEM),
        scratch_shapes=[
            pltpu.VMEM((2, ab // 8, cols), jnp.bfloat16),
            pltpu.VMEM((cols, ab), jnp.bfloat16),
            pltpu.VMEM((32 * KPARTS, ROWS, part), jnp.bfloat16),
            pltpu.VMEM((BLOCK, min(part, 512)), jnp.float32),
            pltpu.VMEM((MPARTS, STEPS * STEP, cols // MPARTS), jnp.bfloat16),
            pltpu.VMEM((STEP, HALF), jnp.float32),
            pltpu.VMEM((STEPS, 2, 4, PIECE, HALF), jnp.float32),
            pltpu.VMEM((STEPS, 2, 3, PIECE, HALF), jnp.float32),
            pltpu.VMEM((STEPS, 2, PIECE, HALF), jnp.float32),
            pltpu.VMEM((2, 3, PIECE, HALF), jnp.float32),
            pltpu.VMEM((2, PIECE, HALF), jnp.float32),
            pltpu.VMEM((PIECE, HALF), jnp.float32),
            pltpu.VMEM((STEPS, 2, 4, 4, PIECE, FINE), jnp.float32),
            pltpu.VMEM((STEPS, 2, 3, 4, PIECE, FINE), jnp.float32),
            pltpu.VMEM((STEPS, 2, 4, PIECE, FINE), jnp.float32),
            pltpu.VMEM((STEPS, 2, 3, PIECE, FINE), jnp.float32),
            pltpu.VMEM((STEPS, 2, PIECE, FINE), jnp.float32),
            pltpu.VMEM((8, PIECE, FINE), jnp.float32),
            pltpu.SemaphoreType.DMA((2,)),
            pltpu.SemaphoreType.DMA,
            pltpu.SemaphoreType.DMA((STEPS, KPARTS)),
            pltpu.SemaphoreType.DMA((STEPS, KPARTS)),
            pltpu.SemaphoreType.DMA((STEPS, 2, KPARTS)),
            pltpu.SemaphoreType.DMA((STEPS, 4, KPARTS)),
            pltpu.SemaphoreType.DMA((STEPS, 2, 3)),
            pltpu.SemaphoreType.DMA((STEPS, 2, 3)),
            pltpu.SemaphoreType.DMA((STEPS, 2)),
            pltpu.SemaphoreType.DMA((2, 3)),
            pltpu.SemaphoreType.DMA,
            pltpu.SemaphoreType.DMA,
            pltpu.SemaphoreType.DMA((STEPS, 2, 3)),
            pltpu.SemaphoreType.DMA((STEPS, 2, 3)),
            pltpu.SemaphoreType.DMA((STEPS, 2, 3)),
            pltpu.SemaphoreType.DMA((STEPS, 2, 3)),
            pltpu.SemaphoreType.DMA((STEPS, 2)),
            pltpu.SemaphoreType.DMA((8,)),
        ],
        compiler_params=pltpu.CompilerParams(
            collective_id=0, has_side_effects=True, vmem_limit_bytes=60 * 2**20
        ),
        cost_estimate=pl.CostEstimate(
            flops=2 * STEPS * STEP * ab * cols, bytes_accessed=2 * ab * cols, transcendentals=0
        ),
        name="ladder",
    )(amplitudes, integrals)


def solution(mesh):
    return jax.shard_map(
        per_device,
        mesh=mesh,
        in_specs=(P(("grp", "col"), None), P("grp", "col")),
        out_specs=P("col", "grp"),
        check_vma=False,
    )
```
